32 devices in a mesh: group: 2 (over y), tensor: 4 (over z), seq: 4 (over x, core).
Axes of the slice: x: 2, y: 2, z: 4, core: 2. Of those that a mesh axis runs over, the one named last changes fastest.
Arguments:
- tokens: bfloat16 [768, 8192], P(('group', 'seq'), 'tensor'), parts along dimension 0, may hold values from -6 to 6
- grad_out: bfloat16 [768, 8192], P(('group', 'seq'), 'tensor'), parts along dimension 0, may hold values from -6 to 6
- counts: int32 [8], P(('group', 'seq')), parts along dimension 0, may hold values from 1 to 96, 288 in all
- packing: int32 [768], P('group'), parts along dimension 0, may hold values from 0 to 383, each once
- gate_weight: bfloat16 [8192, 16384], P('seq', 'tensor'), may hold values from -0.0625 to 0.0625
- up_weight: bfloat16 [8192, 16384], P('seq', 'tensor'), may hold values from -0.0625 to 0.0625
- down_weight: bfloat16 [16384, 8192], P('tensor', 'seq'), may hold values from -0.0625 to 0.0625
Outputs:
- input_grad: bfloat16 [768, 8192], P(('group', 'tensor'), 'seq'), parts along dimension 0
The draws below stay inside these ranges and needn't reach their ends.
There are 2 independent parts, one for each index of `group`. The reference program is written for one: setup_inputs(seed, part) draws one part's arguments, and reference() takes and returns one part's arrays. A program takes and returns all parts, laid end to end along the dimension named above; an argument that names none is the same for every part. Nothing has to cross between parts.
Inputs may be any that keep to these rules, and one draw needn't show every extreme that they name: `packing`: every arriving row index appears exactly once.
All inputs are finite; a program needn't handle non-finite values. No bound on the sum of `counts` on one device may be relied on, other than what follows from the above.
Results may differ from the reference program's by a relative error of at most 0.02.
Values may be sent and summed in bfloat16 or wider, within the bound.
No kernel may reach another device: no remote copies, remote signals or barrier semaphores. Data moves between devices by JAX's collectives and lax.ppermute only.
A program may use at most 192 MiB of HBM per device.

```python
import math
import jax
import jax.numpy as jnp
import numpy as np
from jax import lax

D = 8192
FF = 16384
SHARD_ROWS = 96
ROWS = 384
LIVE = 288
N_TENSOR = 4
N_SEQ = 4


def steps_of(key, dims, shards, low, largest):
    gain, own = 1.0, jax.random.fold_in(key, 6)
    for dim, blocks in shards:
        steps = jnp.exp(jax.random.uniform(jax.random.fold_in(own, dim), (blocks,), jnp.float32, low / len(shards), largest / len(shards)))
        gain = gain * jnp.repeat(steps, dims[dim] // blocks).reshape([-1 if axis == dim else 1 for axis in range(len(dims))])
    return gain


def length_profile(amount, total, reach, slope):
    weights = [(1 << 20) // math.isqrt(grade ** slope) + 1 for grade in range(2, amount + 1)]
    spare, given = total - reach - (amount - 1), [1] * (amount - 1)
    while spare > 0:
        free = [i for i in range(amount - 1) if given[i] < reach]
        pool, remaining = sum([weights[i] for i in free]), spare
        for i in free:
            addition = min(reach - given[i], max(1, remaining * weights[i] // pool), spare)
            given[i] = given[i] + addition
            spare = spare - addition
    return np.array([reach] + given)


def ragged(stream_key, count, total, most, skew):
    if count == 2:
        one = jax.random.randint(stream_key, (), max(1, total - most), min(most, total - 1) + 1)
        return jnp.stack([one, total - one])
    lengths = jnp.asarray(length_profile(count, total, most, skew), jnp.int32)
    pairs = (count - 1) // 2
    giver, receiver = lengths[1:1 + 2 * pairs:2], lengths[2:2 + 2 * pairs:2]
    margin = jnp.minimum(giver - 1, most - receiver)
    shifted = jax.random.randint(jax.random.fold_in(stream_key, 1), (pairs,), 0, 1 << 20) % (margin + 1)
    lengths = lengths.at[1:1 + 2 * pairs:2].set(giver - shifted).at[2:2 + 2 * pairs:2].set(receiver + shifted)
    return lengths[jax.random.permutation(jax.random.fold_in(stream_key, 2), count)]


def gaussian(rng, dims, spread, bound, shards=(), held_as=jnp.bfloat16):
    entries = spread * jax.random.normal(rng, dims, jnp.float32)
    if shards:
        entries = entries * steps_of(rng, dims, shards, -0.22, 0.18)
    return jnp.clip(entries, -bound, bound).astype(held_as)


def setup_inputs(seed: int = 0, part: int = 0) -> dict:
    streams_of = jax.random.split(jax.random.key(seed), 8)
    own_keys = jax.random.split(jax.random.fold_in(streams_of[7], part), 8)
    return {
        "tokens": gaussian(own_keys[0], (ROWS, D), 1.0, 6.0, ((0, 4), (1, 4))),
        "grad_out": gaussian(own_keys[1], (ROWS, D), 1.0, 6.0, ((0, 4), (1, 4))),
        "counts": ragged(own_keys[2], N_SEQ, LIVE, SHARD_ROWS, 2).astype(jnp.int32),
        "packing": jax.random.permutation(own_keys[3], ROWS).astype(jnp.int32),
        "gate_weight": gaussian(streams_of[4], (D, FF), D ** -0.5, 0.0625, ((0, 4), (1, 4))),
        "up_weight": gaussian(streams_of[5], (D, FF), D ** -0.5, 0.0625, ((0, 4), (1, 4))),
        "down_weight": gaussian(streams_of[6], (FF, D), D ** -0.5, 0.0625, ((0, 4), (1, 4))),
    }


def derive(gate, up, hidden_grad):
    sig = jax.nn.sigmoid(gate)
    d_up = (hidden_grad * gate * sig).astype(jnp.bfloat16)
    d_gate = (hidden_grad * up * sig * (1.0 + gate * (1.0 - sig))).astype(jnp.bfloat16)
    return d_gate, d_up


def rounded(value):
    return lax.optimization_barrier(value.astype(jnp.bfloat16)).astype(jnp.float32)


def reference(tokens, grad_out, counts, packing, gate_weight, up_weight, down_weight):
    slot_index = jnp.arange(ROWS, dtype=jnp.int32)
    alive_rows = (slot_index % SHARD_ROWS) < counts[slot_index // SHARD_ROWS]
    masked = jnp.where(alive_rows[:, None], grad_out, jnp.zeros_like(grad_out))
    packed_tokens = tokens[packing]
    packed_cotangent = masked[packing]
    width = D // N_SEQ
    contract = (((1,), (1,)), ((), ()))

    def feature_block(carry, block_index):
        start = (block_index * width).astype(jnp.int32)
        inputs = lax.dynamic_slice_in_dim(packed_tokens, start, width, 1)
        cotangents = lax.dynamic_slice_in_dim(packed_cotangent, start, width, 1)
        gate_rows = lax.dynamic_slice_in_dim(gate_weight, start, width, 0)
        up_rows = lax.dynamic_slice_in_dim(up_weight, start, width, 0)
        down_cols = lax.dynamic_slice_in_dim(down_weight, start, width, 1)
        gate_part = rounded(jnp.dot(inputs, gate_rows, preferred_element_type=jnp.float32))
        up_part = rounded(jnp.dot(inputs, up_rows, preferred_element_type=jnp.float32))
        hidden_part = rounded(lax.dot_general(cotangents, down_cols, contract, preferred_element_type=jnp.float32))
        return (carry[0] + gate_part, carry[1] + up_part, carry[2] + hidden_part), None

    zeros = jnp.zeros((ROWS, FF), jnp.float32)
    (gate, up, hidden_grad), _ = lax.scan(feature_block, (zeros, zeros, zeros), jnp.arange(N_SEQ, dtype=jnp.int32))
    d_gate, d_up = derive(gate, up, hidden_grad)
    fwidth = FF // N_TENSOR

    def hidden_block(carry, block_index):
        start = (block_index * fwidth).astype(jnp.int32)
        gate_grads = lax.dynamic_slice_in_dim(d_gate, start, fwidth, 1)
        up_grads = lax.dynamic_slice_in_dim(d_up, start, fwidth, 1)
        gate_cols = lax.dynamic_slice_in_dim(gate_weight, start, fwidth, 1)
        up_cols = lax.dynamic_slice_in_dim(up_weight, start, fwidth, 1)
        partial_term = lax.dot_general(gate_grads, gate_cols, contract, preferred_element_type=jnp.float32)
        partial_term = partial_term + lax.dot_general(up_grads, up_cols, contract, preferred_element_type=jnp.float32)
        return carry + rounded(partial_term), None

    total, _ = lax.scan(hidden_block, jnp.zeros((ROWS, D), jnp.float32), jnp.arange(N_TENSOR, dtype=jnp.int32))
    return total.astype(jnp.bfloat16)
```

```python
import functools
import jax
import jax.numpy as jnp
from jax import lax
from jax.experimental import pallas as pl
from jax.experimental.pallas import tpu as pltpu
from jax.sharding import PartitionSpec as P

BF, F32 = jnp.bfloat16, jnp.float32
ROW_CONTRACT = (((1,), (1,)), ((), ()))
VMEM = 56 * 1024 * 1024


def derive(gate, up, hidden_grad):
    sig = jax.nn.sigmoid(gate)
    d_up = (hidden_grad * gate * sig).astype(BF)
    d_gate = (hidden_grad * up * sig * (1.0 + gate * (1.0 - sig))).astype(BF)
    return (d_gate, d_up)


def general(tokens, grad_out, counts, packing, gate_weight, up_weight, down_weight):
    shard_rows = tokens.shape[0]
    alive_rows = jnp.arange(shard_rows, dtype=jnp.int32) < counts[0]
    masked = jnp.where(alive_rows[:, None], grad_out, jnp.zeros_like(grad_out))
    whole_tokens, whole_cotangent = (
        lax.all_gather(tokens, "tensor", axis=1, tiled=True),
        lax.all_gather(masked, "tensor", axis=1, tiled=True),
    )
    owned_tokens, owned_cotangent = (
        lax.all_to_all(whole_tokens, "seq", split_axis=1, concat_axis=0, tiled=True),
        lax.all_to_all(whole_cotangent, "seq", split_axis=1, concat_axis=0, tiled=True),
    )
    packed_tokens = jnp.take(owned_tokens, packing, axis=0)
    packed_cotangent = jnp.take(owned_cotangent, packing, axis=0)
    gate_part = jnp.dot(packed_tokens, gate_weight, preferred_element_type=F32)
    up_part = jnp.dot(packed_tokens, up_weight, preferred_element_type=F32)
    hidden_part = lax.dot_general(
        packed_cotangent, down_weight, ROW_CONTRACT, preferred_element_type=F32
    )
    gate, up, hidden_grad = (
        lax.psum(gate_part.astype(BF), "seq").astype(F32),
        lax.psum(up_part.astype(BF), "seq").astype(F32),
        lax.psum(hidden_part.astype(BF), "seq").astype(F32),
    )
    d_gate, d_up = derive(gate, up, hidden_grad)
    result = lax.dot_general(d_gate, gate_weight, ROW_CONTRACT, preferred_element_type=F32)
    return lax.psum_scatter(
        (result + lax.dot_general(d_up, up_weight, ROW_CONTRACT, preferred_element_type=F32)).astype(BF),
        "tensor",
        scatter_dimension=0,
        tiled=True,
    )


def slot_block(slot, half, ids, per_half):
    core, x = ids[0], ids[1]
    which_core = jnp.where(slot % 2 == 0, 1 - core, core)
    which_x = jnp.where(slot // 2 == 0, 1 - x, x)
    return half * per_half + 2 * which_core + which_x


def pick(select_ref, parts, rows_ref):
    width = parts[0].shape[0]
    total = jnp.dot(select_ref[:, :width], parts[0][...], preferred_element_type=F32)
    for k in range(1, len(parts)):
        total += jnp.dot(select_ref[:, k * width:(k + 1) * width], parts[k][...], preferred_element_type=F32)
    rows_ref[...] = total.astype(BF)


def gate_up_kernel(ids, select_ref, p0, p1, p2, p3, gate_ref, up_ref, send_ref, keep_ref, rows_ref):
    slot = pl.program_id(0)

    @pl.when(slot == 0)
    def _():
        pick(select_ref, (p0, p1, p2, p3), rows_ref)

    gate = jnp.dot(rows_ref[...], gate_ref[...], preferred_element_type=F32).astype(BF)
    up = jnp.dot(rows_ref[...], up_ref[...], preferred_element_type=F32).astype(BF)

    @pl.when(slot % 2 == 0)
    def _():
        send_ref[0, 0] = gate
        send_ref[0, 1] = up

    @pl.when(slot % 2 == 1)
    def _():
        keep_ref[0, 0] = gate
        keep_ref[0, 1] = up


def gate_up(half, ids, select, parts, gate_weight, up_weight, block):
    rows, depth = select.shape[0], gate_weight.shape[0]
    whole = lambda a: pl.BlockSpec(a.shape, lambda j, ids: (0,) * a.ndim)
    weight = pl.BlockSpec((depth, block), lambda j, ids: (0, slot_block(j, half, ids, 4)))
    out = pl.BlockSpec((1, 2, rows, block), lambda j, ids: (j // 2, 0, 0, 0))
    return pl.pallas_call(
        gate_up_kernel,
        grid_spec=pltpu.PrefetchScalarGridSpec(
            num_scalar_prefetch=1,
            grid=(4,),
            in_specs=[whole(select)] + [whole(p) for p in parts] + [weight, weight],
            out_specs=[out, out],
            scratch_shapes=[pltpu.VMEM((rows, depth), BF)],
        ),
        out_shape=[jax.ShapeDtypeStruct((2, 2, rows, block), BF)] * 2,
        compiler_params=pltpu.CompilerParams(vmem_limit_bytes=VMEM),
        cost_estimate=pl.CostEstimate(flops=16 * rows * depth * block, bytes_accessed=16 * depth * block, transcendentals=0),
    )(ids, select, *parts, gate_weight, up_weight)


def hidden_kernel(ids, select_ref, p0, p1, p2, p3, down_ref, send_a, send_b, keep_a, keep_b, rows_ref):
    step = pl.program_id(0)
    rows = send_a.shape[2]

    @pl.when(step == 0)
    def _():
        pick(select_ref, (p0, p1, p2, p3), rows_ref)

    hidden = lax.dot_general(rows_ref[...], down_ref[...], ROW_CONTRACT, preferred_element_type=F32).astype(BF)

    @pl.when((step // 2) % 2 == 0)
    def _():
        send_a[0, 0] = hidden[:rows]
        send_b[0, 0] = hidden[rows:]

    @pl.when((step // 2) % 2 == 1)
    def _():
        keep_a[0, 0] = hidden[:rows]
        keep_b[0, 0] = hidden[rows:]


def hidden_grads(ids, select, parts, down_weight, block):
    rows, depth = select.shape[0] // 2, down_weight.shape[1]
    whole = lambda a: pl.BlockSpec(a.shape, lambda j, ids: (0,) * a.ndim)
    weight = pl.BlockSpec((block, depth), lambda j, ids: (slot_block(j // 2, j % 2, ids, 4), 0))

    def sent(j, ids):
        return (j // 4, jnp.where((j // 2) % 2 == 0, j % 2, 1), 0, 0)

    def kept(j, ids):
        slot = j // 2
        return (jnp.where(slot == 3, 1, 0), jnp.where(slot == 0, 0, jnp.where(slot == 2, 1, j % 2)), 0, 0)

    out = lambda place: pl.BlockSpec((1, 1, rows, block), place)
    return pl.pallas_call(
        hidden_kernel,
        grid_spec=pltpu.PrefetchScalarGridSpec(
            num_scalar_prefetch=1,
            grid=(8,),
            in_specs=[whole(select)] + [whole(p) for p in parts] + [weight],
            out_specs=[out(sent), out(sent), out(kept), out(kept)],
            scratch_shapes=[pltpu.VMEM((2 * rows, depth), BF)],
        ),
        out_shape=[jax.ShapeDtypeStruct((2, 2, rows, block), BF)] * 4,
        compiler_params=pltpu.CompilerParams(vmem_limit_bytes=VMEM),
        cost_estimate=pl.CostEstimate(flops=32 * rows * depth * block, bytes_accessed=16 * depth * block, transcendentals=0),
    )(ids, select, *parts, down_weight)


def back_step(mine, other, gate_ref, up_ref, acc, first):
    step = pl.program_id(0)

    def add(source):
        term = lax.dot_general(source[0, step % 2], gate_ref[...], ROW_CONTRACT, preferred_element_type=F32)
        return term + lax.dot_general(source[1, step % 2], up_ref[...], ROW_CONTRACT, preferred_element_type=F32)

    @pl.when(step == 0)
    def _():
        acc[...] = add(mine) if first is None else first[...] + add(mine)

    @pl.when(step == 1)
    def _():
        acc[...] += add(mine)

    @pl.when(step >= 2)
    def _():
        acc[...] += add(other)


def near_kernel(ids, mine, other, gate_ref, up_ref, acc):
    back_step(mine, other, gate_ref, up_ref, acc, None)


def far_kernel(ids, mine, other, gate_ref, up_ref, first, place_ref, o0, o1, o2, o3, acc):
    back_step(mine, other, gate_ref, up_ref, acc, first)

    @pl.when(pl.program_id(0) == 3)
    def _():
        rounded = acc[...].astype(BF)
        for k, out in enumerate((o0, o1, o2, o3)):
            out[...] = jnp.dot(place_ref[k], rounded, preferred_element_type=F32).astype(BF)


def back(far, ids, mine, other, gate_weight, up_weight, block, first=None, place=None):
    rows, depth = mine.shape[2], gate_weight.shape[0]
    whole = lambda a: pl.BlockSpec(a.shape, lambda j, ids: (0,) * a.ndim)

    def spot(j, ids):
        core = jnp.where(j // 2 == 0, ids[0], 1 - ids[0])
        return (0, (j % 2) * 4 + 2 * core + (1 - ids[1] if far else ids[1]))

    weight = pl.BlockSpec((depth, block), spot)
    specs = [whole(mine), whole(other), weight, weight]
    args = (mine, other, gate_weight, up_weight)
    flops = 16 * rows * depth * block
    cost = pl.CostEstimate(flops=flops, bytes_accessed=16 * depth * block, transcendentals=0)
    params = pltpu.CompilerParams(vmem_limit_bytes=VMEM)
    acc = (rows, depth)
    if not far:
        return pl.pallas_call(
            near_kernel,
            grid_spec=pltpu.PrefetchScalarGridSpec(
                num_scalar_prefetch=1, grid=(4,), in_specs=specs,
                out_specs=pl.BlockSpec(acc, lambda j, ids: (0, 0)),
            ),
            out_shape=jax.ShapeDtypeStruct(acc, F32),
            compiler_params=params,
            cost_estimate=cost,
        )(ids, *args)
    piece = (place.shape[1], depth)
    return pl.pallas_call(
        far_kernel,
        grid_spec=pltpu.PrefetchScalarGridSpec(
            num_scalar_prefetch=1, grid=(4,), in_specs=specs + [whole(first), whole(place)],
            out_specs=[pl.BlockSpec(piece, lambda j, ids: (0, 0))] * 4,
            scratch_shapes=[pltpu.VMEM(acc, F32)],
        ),
        out_shape=[jax.ShapeDtypeStruct(piece, BF)] * 4,
        compiler_params=params,
        cost_estimate=cost,
    )(ids, *args, first, place)


def after(value, *others):
    return lax.optimization_barrier((value,) + others)[0]


def tuned(n, tokens, grad_out, counts, packing, gate_weight, up_weight, down_weight):
    shard_rows, depth = tokens.shape
    rows = packing.shape[0]
    live_rows = rows * 3 // 4
    sets, hidden = 2, gate_weight.shape[1]
    block = hidden // 8
    set_rows, piece = live_rows // sets, shard_rows // sets
    t, s = lax.axis_index("tensor"), lax.axis_index("seq")
    core, x = s % 2, s // 2
    ids = jnp.stack([core, x]).astype(jnp.int32)
    sibling = [(i, i ^ 1) for i in range(n)]
    across = [(i, i ^ 2) for i in range(n)]

    def spread(value, k):
        pairs = [(a * n + b, ((b + k) % n) * n + a) for a in range(n) for b in range(n)]
        return lax.ppermute(value, ("tensor", "seq"), pairs)

    token_parts = [spread(tokens, k) for k in range(n)]
    held = after(grad_out, *token_parts)
    grad_parts = [spread(held, k) for k in range(n)]

    all_counts = lax.all_gather(counts, "seq", tiled=True)
    home, place_in = packing // shard_rows, packing % shard_rows
    bound = jnp.sum(jnp.where(home[:, None] == jnp.arange(n)[None, :], all_counts[None, :], 0), axis=1)
    alive = place_in < bound
    order = jnp.arange(rows, dtype=jnp.int32)
    rank = jnp.sum(jnp.where(order[None, :] < order[:, None], alive[None, :].astype(jnp.int32), 0), axis=1)
    index = jnp.where(alive, (rank % sets) * set_rows + rank // sets, -1)
    slot = jnp.arange(rows, dtype=jnp.int32)
    arriving = ((t - slot // shard_rows) % n) * shard_rows + slot % shard_rows
    to_row = (index[None, :] == jnp.arange(live_rows, dtype=jnp.int32)[:, None]).astype(BF)
    from_slot = (packing[:, None] == arriving[None, :]).astype(BF)
    select = jnp.dot(to_row, from_slot, preferred_element_type=F32).astype(BF)
    before = jnp.sum(
        jnp.where(order[None, :] < (jnp.arange(n) * shard_rows)[:, None], alive[None, :].astype(jnp.int32), 0), axis=1
    )
    begin = jnp.stack([(before + sets - 1 - m) // sets for m in range(sets)])
    target = (t + jnp.arange(n)) % n
    target_begin = jnp.sum(
        jnp.where(target[None, :, None] == jnp.arange(n)[None, None, :], begin[:, None, :], 0), axis=2
    )
    place = (
        target_begin[:, :, None, None] + jnp.arange(piece)[None, None, :, None]
        == jnp.arange(set_rows)[None, None, None, :]
    ).astype(BF)
    own = (order // shard_rows == t)
    mine_rank = jnp.sum(jnp.where((order[None, :] == t * shard_rows + jnp.arange(shard_rows)[:, None]),
                                  jnp.where(alive, rank, -1)[None, :], 0), axis=1)
    spot = jnp.where(mine_rank >= 0, (mine_rank % sets) * piece + mine_rank // sets
                     - jnp.where(mine_rank % sets == 0, target_begin[0, 0], target_begin[1, 0]), -1)
    final = (spot[:, None] == jnp.arange(sets * piece)[None, :]).astype(BF)

    gates, ups = [], []
    for half in range(2):
        send, keep = gate_up(half, ids, select, token_parts, gate_weight, up_weight, block)
        got = lax.ppermute(send, "seq", sibling)
        far = (keep[0].astype(F32) + got[0].astype(F32)).astype(BF)
        far_got = lax.ppermute(far, "seq", across)
        near = keep[1].astype(F32) + got[1].astype(F32) + far_got.astype(F32)
        gates.append(near[0])
        ups.append(near[1])

    outs = hidden_grads(ids, select, grad_parts, down_weight, block)
    pieces = []
    for m in range(sets):
        send, keep = outs[m], outs[2 + m]
        got = lax.ppermute(send, "seq", sibling)
        far = (keep[0].astype(F32) + got[0].astype(F32)).astype(BF)
        far_got = lax.ppermute(far, "seq", across)
        hid = keep[1].astype(F32) + got[1].astype(F32) + far_got.astype(F32)
        part = slice(m * set_rows, (m + 1) * set_rows)
        gate = jnp.stack([g[part] for g in gates])
        up = jnp.stack([u[part] for u in ups])
        d = jnp.stack(derive(gate, up, hid))
        d_core = lax.ppermute(d, "seq", sibling)
        d_far = lax.ppermute(d, "seq", across)
        d_both = lax.ppermute(d_far, "seq", sibling)
        first = back(False, ids, d, d_core, gate_weight, up_weight, block)
        parts = back(True, ids, d_far, d_both, gate_weight, up_weight, block, first, place[m])
        total = parts[0].astype(F32)
        for k in range(1, n):
            shift = [(i, (i + k) % n) for i in range(n)]
            total += lax.ppermute(parts[k], "tensor", shift).astype(F32)
        pieces.append(total.astype(BF))
    return jnp.dot(final, jnp.concatenate(pieces), preferred_element_type=F32).astype(BF)


def solution(mesh):
    placed = (
        P(("group", "seq"), "tensor"),
        P(("group", "seq"), "tensor"),
        P(("group", "seq")),
        P("group"),
        P("seq", "tensor"),
        P("seq", "tensor"),
        P("tensor", "seq"),
    )
    if mesh.shape["tensor"] == 4 and mesh.shape["seq"] == 4:
        body = functools.partial(tuned, 4)
    else:
        body = general
    return jax.shard_map(
        body, mesh=mesh, in_specs=placed, out_specs=P(("group", "tensor"), "seq"), check_vma=False
    )
```

```python
import functools
import jax
import jax.numpy as jnp
from jax import lax
from jax.experimental import pallas as pl
from jax.experimental.pallas import tpu as pltpu
from jax.sharding import PartitionSpec as P

BF, F32 = jnp.bfloat16, jnp.float32
ROW_CONTRACT = (((1,), (1,)), ((), ()))
VMEM = 56 * 1024 * 1024
GATE_UP_COST, HIDDEN_COST, NEAR_COST, FAR_COST = 40000000, 60000000, 40000000, 40000000


def derive(gate, up, hidden_grad):
    sig = jax.nn.sigmoid(gate)
    d_up = (hidden_grad * gate * sig).astype(BF)
    d_gate = (hidden_grad * up * sig * (1.0 + gate * (1.0 - sig))).astype(BF)
    return (d_gate, d_up)


def general(tokens, grad_out, counts, packing, gate_weight, up_weight, down_weight):
    shard_rows = tokens.shape[0]
    alive_rows = jnp.arange(shard_rows, dtype=jnp.int32) < counts[0]
    masked = jnp.where(alive_rows[:, None], grad_out, jnp.zeros_like(grad_out))
    whole_tokens, whole_cotangent = (
        lax.all_gather(tokens, "tensor", axis=1, tiled=True),
        lax.all_gather(masked, "tensor", axis=1, tiled=True),
    )
    owned_tokens, owned_cotangent = (
        lax.all_to_all(whole_tokens, "seq", split_axis=1, concat_axis=0, tiled=True),
        lax.all_to_all(whole_cotangent, "seq", split_axis=1, concat_axis=0, tiled=True),
    )
    packed_tokens = jnp.take(owned_tokens, packing, axis=0)
    packed_cotangent = jnp.take(owned_cotangent, packing, axis=0)
    gate_part = jnp.dot(packed_tokens, gate_weight, preferred_element_type=F32)
    up_part = jnp.dot(packed_tokens, up_weight, preferred_element_type=F32)
    hidden_part = lax.dot_general(
        packed_cotangent, down_weight, ROW_CONTRACT, preferred_element_type=F32
    )
    gate, up, hidden_grad = (
        lax.psum(gate_part.astype(BF), "seq").astype(F32),
        lax.psum(up_part.astype(BF), "seq").astype(F32),
        lax.psum(hidden_part.astype(BF), "seq").astype(F32),
    )
    d_gate, d_up = derive(gate, up, hidden_grad)
    result = lax.dot_general(d_gate, gate_weight, ROW_CONTRACT, preferred_element_type=F32)
    return lax.psum_scatter(
        (result + lax.dot_general(d_up, up_weight, ROW_CONTRACT, preferred_element_type=F32)).astype(BF),
        "tensor",
        scatter_dimension=0,
        tiled=True,
    )


def region(ref, axis, index, size):
    spot = pl.ds(pl.multiple_of(index * size, size), size)
    return ref.at[spot] if axis == 0 else ref.at[:, spot]


def slot_index(slot, core, x):
    which_core = 1 - core if slot % 2 == 0 else core
    which_x = 1 - x if slot // 2 == 0 else x
    return which_x * 2 + which_core


def start(source, target, sem):
    copy = pltpu.make_async_copy(source, target, sem)
    copy.start()
    return copy


class Stream:
    def __init__(self, copies, ahead):
        self.copies, self.ahead, self.begun = copies, ahead, 0
        self.reach(0)

    def reach(self, index):
        while self.begun < min(index + self.ahead, len(self.copies)):
            for copy in self.copies[self.begun]:
                copy.start()
            self.begun += 1

    def wait(self, index):
        for copy in self.copies[index]:
            copy.wait()
        self.reach(index + 1)


IN_VMEM = pl.BlockSpec(memory_space=pltpu.VMEM)
IN_HBM = pl.BlockSpec(memory_space=pl.ANY)
IN_SMEM = pl.BlockSpec(memory_space=pltpu.SMEM)


def call(kernel, in_specs, out_shape, scratch, cost):
    return pl.pallas_call(
        kernel,
        in_specs=in_specs,
        out_specs=[IN_HBM] * len(out_shape),
        out_shape=[jax.ShapeDtypeStruct(shape, dtype) for shape, dtype in out_shape],
        scratch_shapes=scratch,
        compiler_params=pltpu.CompilerParams(vmem_limit_bytes=VMEM),
        cost_estimate=pl.CostEstimate(flops=0, bytes_accessed=cost, transcendentals=0),
    )


def pick_start(parts, arrived, sems):
    width = parts[0].shape[0]
    return [start(part, arrived.at[pl.ds(k * width, width)], sems.at[k]) for k, part in enumerate(parts)]


def pick_end(moves, select_ref, arrived, rows_v):
    for move in moves:
        move.wait()
    rows_v[...] = jnp.dot(select_ref[...], arrived[...], preferred_element_type=F32).astype(BF)


def gate_up_kernel(ids, select_ref, p0, p1, p2, p3, gate_w, up_w, send_far, keep_far, send_near, keep_near,
                   gate_v, up_v, out_v, rows_v, arrived, sems):
    core, x = ids[0], ids[1]
    block = gate_v.shape[2]
    moves = pick_start((p0, p1, p2, p3), arrived, sems.at[0])
    loads = []
    for slot in range(4):
        index = slot_index(slot, core, x)
        for a, (weight, held) in enumerate(((gate_w, gate_v), (up_w, up_v))):
            loads.append([pltpu.make_async_copy(region(weight, 1, index, block), held.at[slot], sems.at[1 + a, slot])])
    loads = Stream(loads, 3)
    pick_end(moves, select_ref, arrived, rows_v)
    stores = []
    for slot, out in enumerate((send_far, keep_far, send_near, keep_near)):
        for a, held in enumerate((gate_v, up_v)):
            loads.wait(2 * slot + a)
            out_v[slot, a] = jnp.dot(rows_v[...], held[slot], preferred_element_type=F32).astype(BF)
            stores.append(start(out_v.at[slot, a], out.at[a], sems.at[3 + a, slot]))
    for store in stores:
        store.wait()


def gate_up(ids, select, parts, gate_weight, up_weight):
    depth, block = gate_weight.shape[0], gate_weight.shape[1] // 4
    count = select.shape[0]
    return call(
        gate_up_kernel,
        [IN_SMEM, IN_VMEM] + [IN_HBM] * 6,
        [((2, count, block), BF)] * 4,
        [pltpu.VMEM((4, depth, block), BF)] * 2 + [
            pltpu.VMEM((4, 2, count, block), BF),
            pltpu.VMEM((count, depth), BF),
            pltpu.VMEM((select.shape[1], depth), BF),
            pltpu.SemaphoreType.DMA((5, 4)),
        ],
        GATE_UP_COST,
    )(ids, select, *parts, gate_weight, up_weight)


def hidden_kernel(ids, select_ref, p0, p1, p2, p3, down, send_a, send_b, keep_a, keep_b,
                  down_v, out_v, rows_v, arrived, sems):
    core, x = ids[0], ids[1]
    rows, block = send_a.shape[1], send_a.shape[2]
    moves = pick_start((p0, p1, p2, p3), arrived, sems.at[0])
    loads = Stream(
        [[pltpu.make_async_copy(region(down, 0, slot_index(slot, core, x), block), down_v.at[slot], sems.at[1, slot])]
         for slot in range(4)], 3)
    pick_end(moves, select_ref, arrived, rows_v)
    stores = []
    for slot in range(4):
        loads.wait(slot)
        hidden = lax.dot_general(rows_v[...], down_v[slot], ROW_CONTRACT, preferred_element_type=F32)
        out_v[slot] = hidden.astype(BF)
        for m, out in enumerate((send_a, send_b) if slot % 2 == 0 else (keep_a, keep_b)):
            stores.append(start(out_v.at[slot, pl.ds(m * rows, rows)], out.at[slot // 2], sems.at[2 + m, slot]))
    for store in stores:
        store.wait()


def hidden_grads(ids, select, parts, down_weight):
    depth, block = down_weight.shape[1], down_weight.shape[0] // 4
    count = select.shape[0]
    return call(
        hidden_kernel,
        [IN_SMEM, IN_VMEM] + [IN_HBM] * 5,
        [((2, count // 2, block), BF)] * 4,
        [
            pltpu.VMEM((4, block, depth), BF),
            pltpu.VMEM((4, count, block), BF),
            pltpu.VMEM((count, depth), BF),
            pltpu.VMEM((select.shape[1], depth), BF),
            pltpu.SemaphoreType.DMA((4, 4)),
        ],
        HIDDEN_COST,
    )(ids, select, *parts, down_weight)


CHUNKS = 4


def back_begin(core, which_x, pairs, gate_w, up_w, grads_v, weight_v, sems, grad_sems):
    rows, block = pairs[0][0].shape[1], pairs[0][0].shape[2]
    height, width = gate_w.shape[0] // CHUNKS, 2 * block
    moves = []
    for m, pair in enumerate(pairs):
        for source, value in enumerate(pair):
            which_core = core if source == 0 else 1 - core
            spot = pl.ds(pl.multiple_of(which_core * block, block), block)
            for a in range(2):
                moves.append(start(value.at[a], grads_v.at[a, pl.ds(m * rows, rows), spot],
                                   grad_sems.at[m, 2 * source + a]))
    side = pl.ds(pl.multiple_of(which_x * width, width), width)
    loads = []
    for chunk in range(CHUNKS):
        high = pl.ds(chunk * height, height)
        loads.append([
            pltpu.make_async_copy(weight.at[high, side], weight_v.at[a, high], sems.at[chunk, a])
            for a, weight in enumerate((gate_w, up_w))
        ])
    return moves, Stream(loads, 2)


def back_chunk(chunk, grads_v, weight_v, loads):
    height = weight_v.shape[1] // CHUNKS
    spot = pl.ds(chunk * height, height)
    loads.wait(chunk)
    total = lax.dot_general(grads_v[0], weight_v[0, spot], ROW_CONTRACT, preferred_element_type=F32)
    return total + lax.dot_general(grads_v[1], weight_v[1, spot], ROW_CONTRACT, preferred_element_type=F32)


def near_kernel(ids, mine_a, other_a, mine_b, other_b, gate_w, up_w, out_a, out_b,
                grads_v, weight_v, out_v, sems, grad_sems, out_sems):
    moves, loads = back_begin(ids[0], ids[1], ((mine_a, other_a), (mine_b, other_b)), gate_w, up_w,
                              grads_v, weight_v, sems, grad_sems)
    height, rows = gate_w.shape[0] // CHUNKS, out_a.shape[0]
    for move in moves:
        move.wait()
    stores = []
    for chunk in range(CHUNKS):
        spot = pl.ds(chunk * height, height)
        out_v[:, spot] = back_chunk(chunk, grads_v, weight_v, loads)
        for m, out in enumerate((out_a, out_b)):
            stores.append(start(out_v.at[pl.ds(m * rows, rows), spot], out.at[:, spot], out_sems.at[chunk, m]))
    for store in stores:
        store.wait()


def far_kernel(ids, place_ref, mine, other, gate_w, up_w, first, o0, o1, o2, o3,
               grads_v, weight_v, first_v, out_v, sems, grad_sems, out_sems, first_sem):
    moves, loads = back_begin(ids[0], 1 - ids[1], ((mine, other),), gate_w, up_w, grads_v, weight_v, sems, grad_sems)
    moves.append(start(first, first_v, first_sem.at[0]))
    height = gate_w.shape[0] // CHUNKS
    piece = o0.shape[0]
    for move in moves:
        move.wait()
    stores = []
    for chunk in range(CHUNKS):
        spot = pl.ds(chunk * height, height)
        total = first_v[:, spot] + back_chunk(chunk, grads_v, weight_v, loads)
        out_v[:, spot] = jnp.dot(place_ref[...], total.astype(BF), preferred_element_type=F32).astype(BF)
        for k, out in enumerate((o0, o1, o2, o3)):
            part = out_v.at[pl.ds(k * piece, piece), spot]
            stores.append(start(part, out.at[:, spot], out_sems.at[chunk, k]))
    for store in stores:
        store.wait()


def near(ids, mine, other, gate_weight, up_weight):
    sets, rows, block, depth = len(mine), mine[0].shape[1], mine[0].shape[2], gate_weight.shape[0]
    count = sets * rows
    return call(
        near_kernel,
        [IN_SMEM] + [IN_HBM] * 6,
        [((rows, depth), F32)] * 2,
        [
            pltpu.VMEM((2, count, 2 * block), BF),
            pltpu.VMEM((2, depth, 2 * block), BF),
            pltpu.VMEM((count, depth), F32),
            pltpu.SemaphoreType.DMA((CHUNKS, 2)),
            pltpu.SemaphoreType.DMA((sets, 4)),
            pltpu.SemaphoreType.DMA((CHUNKS, sets)),
        ],
        NEAR_COST,
    )(ids, mine[0], other[0], mine[1], other[1], gate_weight, up_weight)


def far(ids, place, mine, other, gate_weight, up_weight, first):
    rows, block, depth = mine.shape[1], mine.shape[2], gate_weight.shape[0]
    count = place.shape[0]
    return call(
        far_kernel,
        [IN_SMEM, IN_VMEM] + [IN_HBM] * 5,
        [((count // 4, depth), BF)] * 4,
        [
            pltpu.VMEM((2, rows, 2 * block), BF),
            pltpu.VMEM((2, depth, 2 * block), BF),
            pltpu.VMEM((rows, depth), F32),
            pltpu.VMEM((count, depth), BF),
            pltpu.SemaphoreType.DMA((CHUNKS, 2)),
            pltpu.SemaphoreType.DMA((1, 4)),
            pltpu.SemaphoreType.DMA((CHUNKS, 4)),
            pltpu.SemaphoreType.DMA((1,)),
        ],
        FAR_COST,
    )(ids, place, mine, other, gate_weight, up_weight, first)


def after(value, *others):
    return lax.optimization_barrier((value,) + others)[0]


def tuned(n, tokens, grad_out, counts, packing, gate_weight, up_weight, down_weight):
    shard_rows, depth = tokens.shape
    rows = packing.shape[0]
    live_rows = rows * 3 // 4
    sets = 2
    set_rows, piece = live_rows // sets, shard_rows // sets
    t, s = lax.axis_index("tensor"), lax.axis_index("seq")
    core, x = s % 2, s // 2
    ids = jnp.stack([core, x]).astype(jnp.int32)
    sibling = [(i, i ^ 1) for i in range(n)]
    across = [(i, i ^ 2) for i in range(n)]

    def spread(value, k):
        pairs = [(a * n + b, ((b + k) % n) * n + a) for a in range(n) for b in range(n)]
        return lax.ppermute(value, ("tensor", "seq"), pairs)

    token_parts = [spread(tokens, k) for k in range(n)]
    held = after(grad_out, *token_parts)
    grad_parts = [spread(held, k) for k in range(n)]

    all_counts = lax.all_gather(counts, "seq", tiled=True)
    home, place_in = packing // shard_rows, packing % shard_rows
    bound = jnp.sum(jnp.where(home[:, None] == jnp.arange(n)[None, :], all_counts[None, :], 0), axis=1)
    alive = place_in < bound
    order = jnp.arange(rows, dtype=jnp.int32)
    rank = jnp.sum(jnp.where(order[None, :] < order[:, None], alive[None, :].astype(jnp.int32), 0), axis=1)
    index = jnp.where(alive, (rank % sets) * set_rows + rank // sets, -1)
    slot = jnp.arange(rows, dtype=jnp.int32)
    arriving = ((t - slot // shard_rows) % n) * shard_rows + slot % shard_rows
    to_row = (index[None, :] == jnp.arange(live_rows, dtype=jnp.int32)[:, None]).astype(BF)
    from_slot = (packing[:, None] == arriving[None, :]).astype(BF)
    select = jnp.dot(to_row, from_slot, preferred_element_type=F32).astype(BF)
    before = jnp.sum(
        jnp.where(order[None, :] < (jnp.arange(n) * shard_rows)[:, None], alive[None, :].astype(jnp.int32), 0), axis=1
    )
    begin = jnp.stack([(before + sets - 1 - m) // sets for m in range(sets)])
    target = (t + jnp.arange(n)) % n
    target_begin = jnp.sum(
        jnp.where(target[None, :, None] == jnp.arange(n)[None, None, :], begin[:, None, :], 0), axis=2
    )
    place = (
        target_begin[:, :, None, None] + jnp.arange(piece)[None, None, :, None]
        == jnp.arange(set_rows)[None, None, None, :]
    ).astype(BF)
    own = (order // shard_rows == t)
    mine_rank = jnp.sum(jnp.where((order[None, :] == t * shard_rows + jnp.arange(shard_rows)[:, None]),
                                  jnp.where(alive, rank, -1)[None, :], 0), axis=1)
    spot = jnp.where(mine_rank >= 0, (mine_rank % sets) * piece + mine_rank // sets
                     - jnp.where(mine_rank % sets == 0, target_begin[0, 0], target_begin[1, 0]), -1)
    final = (spot[:, None] == jnp.arange(sets * piece)[None, :]).astype(BF)

    def project(ids, select, gate_weight, up_weight, *token_parts):
        send_far, keep_far, send_near, keep_near = gate_up(ids, select, token_parts, gate_weight, up_weight)
        got_far = lax.ppermute(send_far, "seq", sibling)
        return (keep_far.astype(F32) + got_far.astype(F32)).astype(BF), send_near, keep_near

    def absent(ids, select, *rest):
        nothing = jnp.zeros((2, live_rows, gate_weight.shape[1] // 4), BF)
        return nothing, nothing, nothing

    pair_far, send_near, keep_near = lax.cond(
        packing[0] >= 0, project, absent, ids, select, gate_weight, up_weight, *token_parts
    )

    across_near = lax.ppermute(pair_far, "seq", across)

    outs = hidden_grads(ids, after(select, pair_far), grad_parts, down_weight)
    got_near = lax.ppermute(after(send_near, outs[0]), "seq", sibling)
    gate_near = keep_near.astype(F32) + got_near.astype(F32) + across_near.astype(F32)
    ds, ds_core = [], []
    for m in range(sets):
        send, keep = outs[m], outs[sets + m]
        got = lax.ppermute(send, "seq", sibling)
        pair_far = (keep[0].astype(F32) + got[0].astype(F32)).astype(BF)
        hid = keep[1].astype(F32) + got[1].astype(F32) + lax.ppermute(pair_far, "seq", across).astype(F32)
        part = slice(m * set_rows, (m + 1) * set_rows)
        ds.append(jnp.stack(derive(gate_near[0, part], gate_near[1, part], hid)))
        ds_core.append(lax.ppermute(ds[m], "seq", sibling))
    ds_far = [lax.ppermute(d, "seq", across) for d in ds]
    firsts = near(ids, ds, ds_core, gate_weight, up_weight)
    pieces = []
    for m in range(sets):
        d_both = lax.ppermute(after(ds_far[m], firsts[0]), "seq", sibling)
        parts = far(ids, place[m].reshape(n * piece, set_rows), ds_far[m], d_both, gate_weight, up_weight, firsts[m])
        total = parts[0].astype(F32)
        for k in range(1, n):
            shift = [(i, (i + k) % n) for i in range(n)]
            total += lax.ppermute(parts[k], "tensor", shift).astype(F32)
        pieces.append(total.astype(BF))
    return jnp.dot(final, jnp.concatenate(pieces), preferred_element_type=F32).astype(BF)


def solution(mesh):
    placed = (
        P(("group", "seq"), "tensor"),
        P(("group", "seq"), "tensor"),
        P(("group", "seq")),
        P("group"),
        P("seq", "tensor"),
        P("seq", "tensor"),
        P("tensor", "seq"),
    )
    if mesh.shape["tensor"] == 4 and mesh.shape["seq"] == 4:
        body = functools.partial(tuned, 4)
    else:
        body = general
    return jax.shard_map(
        body, mesh=mesh, in_specs=placed, out_specs=P(("group", "tensor"), "seq"), check_vma=False
    )
```

```python
import functools
import jax
import jax.numpy as jnp
from jax import lax
from jax.experimental import pallas as pl
from jax.experimental.pallas import tpu as pltpu
from jax.sharding import PartitionSpec as P

BF, F32 = jnp.bfloat16, jnp.float32
ROW_CONTRACT = (((1,), (1,)), ((), ()))
VMEM = 49 * 1024 * 1024
GATE_UP_COST, HIDDEN_COST, NEAR_COST, FAR_COST = 40000000, 60000000, 40000000, 40000000


def derive(gate, up, hidden_grad):
    sig = jax.nn.sigmoid(gate)
    d_up = (hidden_grad * gate * sig).astype(BF)
    d_gate = (hidden_grad * up * sig * (1.0 + gate * (1.0 - sig))).astype(BF)
    return (d_gate, d_up)


def general(tokens, grad_out, counts, packing, gate_weight, up_weight, down_weight):
    shard_rows = tokens.shape[0]
    alive_rows = jnp.arange(shard_rows, dtype=jnp.int32) < counts[0]
    masked = jnp.where(alive_rows[:, None], grad_out, jnp.zeros_like(grad_out))
    whole_tokens, whole_cotangent = (
        lax.all_gather(tokens, "tensor", axis=1, tiled=True),
        lax.all_gather(masked, "tensor", axis=1, tiled=True),
    )
    owned_tokens, owned_cotangent = (
        lax.all_to_all(whole_tokens, "seq", split_axis=1, concat_axis=0, tiled=True),
        lax.all_to_all(whole_cotangent, "seq", split_axis=1, concat_axis=0, tiled=True),
    )
    packed_tokens = jnp.take(owned_tokens, packing, axis=0)
    packed_cotangent = jnp.take(owned_cotangent, packing, axis=0)
    gate_part = jnp.dot(packed_tokens, gate_weight, preferred_element_type=F32)
    up_part = jnp.dot(packed_tokens, up_weight, preferred_element_type=F32)
    hidden_part = lax.dot_general(
        packed_cotangent, down_weight, ROW_CONTRACT, preferred_element_type=F32
    )
    gate, up, hidden_grad = (
        lax.psum(gate_part.astype(BF), "seq").astype(F32),
        lax.psum(up_part.astype(BF), "seq").astype(F32),
        lax.psum(hidden_part.astype(BF), "seq").astype(F32),
    )
    d_gate, d_up = derive(gate, up, hidden_grad)
    result = lax.dot_general(d_gate, gate_weight, ROW_CONTRACT, preferred_element_type=F32)
    return lax.psum_scatter(
        (result + lax.dot_general(d_up, up_weight, ROW_CONTRACT, preferred_element_type=F32)).astype(BF),
        "tensor",
        scatter_dimension=0,
        tiled=True,
    )


def region(ref, axis, index, size):
    spot = pl.ds(pl.multiple_of(index * size, size), size)
    return ref.at[spot] if axis == 0 else ref.at[:, spot]


def slot_index(slot, core, x):
    which_core = 1 - core if slot % 2 == 0 else core
    which_x = 1 - x if slot // 2 == 0 else x
    return which_x * 2 + which_core


def start(source, target, sem):
    copy = pltpu.make_async_copy(source, target, sem)
    copy.start()
    return copy


class Stream:
    def __init__(self, copies, ahead):
        self.copies, self.ahead, self.begun = copies, ahead, 0
        self.reach(0)

    def reach(self, index):
        while self.begun < min(index + self.ahead, len(self.copies)):
            for copy in self.copies[self.begun]:
                copy.start()
            self.begun += 1

    def wait(self, index):
        for copy in self.copies[index]:
            copy.wait()
        self.reach(index + 1)


IN_VMEM = pl.BlockSpec(memory_space=pltpu.VMEM)
IN_HBM = pl.BlockSpec(memory_space=pl.ANY)
IN_SMEM = pl.BlockSpec(memory_space=pltpu.SMEM)


def call(kernel, in_specs, out_shape, scratch, cost):
    return pl.pallas_call(
        kernel,
        in_specs=in_specs,
        out_specs=[IN_HBM] * len(out_shape),
        out_shape=[jax.ShapeDtypeStruct(shape, dtype) for shape, dtype in out_shape],
        scratch_shapes=scratch,
        compiler_params=pltpu.CompilerParams(vmem_limit_bytes=VMEM),
        cost_estimate=pl.CostEstimate(flops=0, bytes_accessed=cost, transcendentals=0),
    )


def pick_start(parts, arrived, sems):
    width = parts[0].shape[0]
    return [start(part, arrived.at[pl.ds(k * width, width)], sems.at[k]) for k, part in enumerate(parts)]


def pick_end(moves, select_ref, arrived, rows_v):
    for move in moves:
        move.wait()
    rows_v[...] = jnp.dot(select_ref[...], arrived[...], preferred_element_type=F32).astype(BF)


def gate_up_kernel(ids, select_ref, p0, p1, p2, p3, gate_w, up_w, send_far, keep_far, send_near, keep_near,
                   gate_v, up_v, out_v, rows_v, arrived, sems):
    core, x = ids[0], ids[1]
    block = gate_v.shape[2]
    moves = pick_start((p0, p1, p2, p3), arrived, sems.at[0])
    loads = []
    for slot in range(4):
        index = slot_index(slot, core, x)
        for a, (weight, held) in enumerate(((gate_w, gate_v), (up_w, up_v))):
            loads.append([pltpu.make_async_copy(region(weight, 1, index, block), held.at[slot], sems.at[1 + a, slot])])
    loads = Stream(loads, 3)
    pick_end(moves, select_ref, arrived, rows_v)
    stores = []
    for slot, out in enumerate((send_far, keep_far, send_near, keep_near)):
        for a, held in enumerate((gate_v, up_v)):
            loads.wait(2 * slot + a)
            out_v[slot, a] = jnp.dot(rows_v[...], held[slot], preferred_element_type=F32).astype(BF)
            stores.append(start(out_v.at[slot, a], out.at[a], sems.at[3 + a, slot]))
    for store in stores:
        store.wait()


def gate_up(ids, select, parts, gate_weight, up_weight):
    depth, block = gate_weight.shape[0], gate_weight.shape[1] // 4
    count = select.shape[0]
    return call(
        gate_up_kernel,
        [IN_SMEM, IN_VMEM] + [IN_HBM] * 6,
        [((2, count, block), BF)] * 4,
        [pltpu.VMEM((4, depth, block), BF)] * 2 + [
            pltpu.VMEM((4, 2, count, block), BF),
            pltpu.VMEM((count, depth), BF),
            pltpu.VMEM((select.shape[1], depth), BF),
            pltpu.SemaphoreType.DMA((5, 4)),
        ],
        GATE_UP_COST,
    )(ids, select, *parts, gate_weight, up_weight)


def hidden_kernel(ids, select_ref, p0, p1, p2, p3, down, send_a, send_b, keep_a, keep_b,
                  down_v, out_v, rows_v, arrived, sems):
    core, x = ids[0], ids[1]
    rows, block = send_a.shape[1], send_a.shape[2]
    moves = pick_start((p0, p1, p2, p3), arrived, sems.at[0])
    loads = Stream(
        [[pltpu.make_async_copy(region(down, 0, slot_index(slot, core, x), block), down_v.at[slot], sems.at[1, slot])]
         for slot in range(4)], 3)
    pick_end(moves, select_ref, arrived, rows_v)
    stores = []
    for slot in range(4):
        loads.wait(slot)
        hidden = lax.dot_general(rows_v[...], down_v[slot], ROW_CONTRACT, preferred_element_type=F32)
        out_v[slot] = hidden.astype(BF)
        for m, out in enumerate((send_a, send_b) if slot % 2 == 0 else (keep_a, keep_b)):
            stores.append(start(out_v.at[slot, pl.ds(m * rows, rows)], out.at[slot // 2], sems.at[2 + m, slot]))
    for store in stores:
        store.wait()


def hidden_grads(ids, select, parts, down_weight):
    depth, block = down_weight.shape[1], down_weight.shape[0] // 4
    count = select.shape[0]
    return call(
        hidden_kernel,
        [IN_SMEM, IN_VMEM] + [IN_HBM] * 5,
        [((2, count // 2, block), BF)] * 4,
        [
            pltpu.VMEM((4, block, depth), BF),
            pltpu.VMEM((4, count, block), BF),
            pltpu.VMEM((count, depth), BF),
            pltpu.VMEM((select.shape[1], depth), BF),
            pltpu.SemaphoreType.DMA((4, 4)),
        ],
        HIDDEN_COST,
    )(ids, select, *parts, down_weight)


CHUNKS = 4


def back_begin(core, which_x, pairs, gate_w, up_w, grads_v, weight_v, sems, grad_sems):
    rows, block = pairs[0][0].shape[1], pairs[0][0].shape[2]
    height, width = gate_w.shape[0] // CHUNKS, 2 * block
    moves = []
    for m, pair in enumerate(pairs):
        for source, value in enumerate(pair):
            which_core = core if source == 0 else 1 - core
            spot = pl.ds(pl.multiple_of(which_core * block, block), block)
            for a in range(2):
                moves.append(start(value.at[a], grads_v.at[a, pl.ds(m * rows, rows), spot],
                                   grad_sems.at[m, 2 * source + a]))
    side = pl.ds(pl.multiple_of(which_x * width, width), width)
    loads = []
    for chunk in range(CHUNKS):
        high = pl.ds(chunk * height, height)
        loads.append([
            pltpu.make_async_copy(weight.at[high, side], weight_v.at[a, high], sems.at[chunk, a])
            for a, weight in enumerate((gate_w, up_w))
        ])
    return moves, Stream(loads, 2)


def back_chunk(chunk, grads_v, weight_v, loads):
    height = weight_v.shape[1] // CHUNKS
    spot = pl.ds(chunk * height, height)
    loads.wait(chunk)
    total = lax.dot_general(grads_v[0], weight_v[0, spot], ROW_CONTRACT, preferred_element_type=F32)
    return total + lax.dot_general(grads_v[1], weight_v[1, spot], ROW_CONTRACT, preferred_element_type=F32)


def near_kernel(ids, mine_a, other_a, mine_b, other_b, gate_w, up_w, out_a, out_b,
                grads_v, weight_v, out_v, sems, grad_sems, out_sems):
    moves, loads = back_begin(ids[0], ids[1], ((mine_a, other_a), (mine_b, other_b)), gate_w, up_w,
                              grads_v, weight_v, sems, grad_sems)
    height, rows = gate_w.shape[0] // CHUNKS, out_a.shape[0]
    for move in moves:
        move.wait()
    stores = []
    for chunk in range(CHUNKS):
        spot = pl.ds(chunk * height, height)
        out_v[:, spot] = back_chunk(chunk, grads_v, weight_v, loads)
        for m, out in enumerate((out_a, out_b)):
            stores.append(start(out_v.at[pl.ds(m * rows, rows), spot], out.at[:, spot], out_sems.at[chunk, m]))
    for store in stores:
        store.wait()


def far_kernel(ids, place_ref, mine, other, gate_w, up_w, first, o0, o1, o2, o3,
               grads_v, weight_v, first_v, out_v, sems, grad_sems, out_sems, first_sem):
    begun = start(first, first_v, first_sem.at[0])
    moves, loads = back_begin(ids[0], 1 - ids[1], ((mine, other),), gate_w, up_w, grads_v, weight_v, sems, grad_sems)
    height = gate_w.shape[0] // CHUNKS
    piece = o0.shape[0]
    for move in [begun] + moves:
        move.wait()
    stores = []
    for chunk in range(CHUNKS):
        spot = pl.ds(chunk * height, height)
        total = first_v[:, spot] + back_chunk(chunk, grads_v, weight_v, loads)
        out_v[:, spot] = jnp.dot(place_ref[...], total.astype(BF), preferred_element_type=F32).astype(BF)
        for k, out in enumerate((o0, o1, o2, o3)):
            part = out_v.at[pl.ds(k * piece, piece), spot]
            stores.append(start(part, out.at[:, spot], out_sems.at[chunk, k]))
    for store in stores:
        store.wait()


def near(ids, mine, other, gate_weight, up_weight):
    sets, rows, block, depth = len(mine), mine[0].shape[1], mine[0].shape[2], gate_weight.shape[0]
    count = sets * rows
    return call(
        near_kernel,
        [IN_SMEM] + [IN_HBM] * 6,
        [((rows, depth), F32)] * 2,
        [
            pltpu.VMEM((2, count, 2 * block), BF),
            pltpu.VMEM((2, depth, 2 * block), BF),
            pltpu.VMEM((count, depth), F32),
            pltpu.SemaphoreType.DMA((CHUNKS, 2)),
            pltpu.SemaphoreType.DMA((sets, 4)),
            pltpu.SemaphoreType.DMA((CHUNKS, sets)),
        ],
        NEAR_COST,
    )(ids, mine[0], other[0], mine[1], other[1], gate_weight, up_weight)


def far(ids, place, mine, other, gate_weight, up_weight, first):
    rows, block, depth = mine.shape[1], mine.shape[2], gate_weight.shape[0]
    count = place.shape[0]
    return call(
        far_kernel,
        [IN_SMEM, IN_VMEM] + [IN_HBM] * 5,
        [((count // 4, depth), BF)] * 4,
        [
            pltpu.VMEM((2, rows, 2 * block), BF),
            pltpu.VMEM((2, depth, 2 * block), BF),
            pltpu.VMEM((rows, depth), F32),
            pltpu.VMEM((count, depth), BF),
            pltpu.SemaphoreType.DMA((CHUNKS, 2)),
            pltpu.SemaphoreType.DMA((1, 4)),
            pltpu.SemaphoreType.DMA((CHUNKS, 4)),
            pltpu.SemaphoreType.DMA((1,)),
        ],
        FAR_COST,
    )(ids, place, mine, other, gate_weight, up_weight, first)


def after(value, *others):
    return lax.optimization_barrier((value,) + others)[0]


def tuned(n, tokens, grad_out, counts, packing, gate_weight, up_weight, down_weight):
    shard_rows, depth = tokens.shape
    rows = packing.shape[0]
    live_rows = rows * 3 // 4
    sets = 2
    set_rows, piece = live_rows // sets, shard_rows // sets
    t, s = lax.axis_index("tensor"), lax.axis_index("seq")
    core, x = s % 2, s // 2
    ids = jnp.stack([core, x]).astype(jnp.int32)
    sibling = [(i, i ^ 1) for i in range(n)]
    across = [(i, i ^ 2) for i in range(n)]

    def spread(value, k):
        pairs = [(a * n + b, ((b + k) % n) * n + a) for a in range(n) for b in range(n)]
        return lax.ppermute(value, ("tensor", "seq"), pairs)

    token_parts = [spread(tokens, k) for k in range(n)]

    all_counts = lax.all_gather(counts, "seq", tiled=True)
    home, place_in = packing // shard_rows, packing % shard_rows
    bound = jnp.sum(jnp.where(home[:, None] == jnp.arange(n)[None, :], all_counts[None, :], 0), axis=1)
    alive = place_in < bound
    order = jnp.arange(rows, dtype=jnp.int32)
    rank = jnp.sum(jnp.where(order[None, :] < order[:, None], alive[None, :].astype(jnp.int32), 0), axis=1)
    index = jnp.where(alive, (rank % sets) * set_rows + rank // sets, -1)
    slot = jnp.arange(rows, dtype=jnp.int32)
    arriving = ((t - slot // shard_rows) % n) * shard_rows + slot % shard_rows
    to_row = (index[None, :] == jnp.arange(live_rows, dtype=jnp.int32)[:, None]).astype(BF)
    from_slot = (packing[:, None] == arriving[None, :]).astype(BF)
    select = jnp.dot(to_row, from_slot, preferred_element_type=F32).astype(BF)
    before = jnp.sum(
        jnp.where(order[None, :] < (jnp.arange(n) * shard_rows)[:, None], alive[None, :].astype(jnp.int32), 0), axis=1
    )
    begin = jnp.stack([(before + sets - 1 - m) // sets for m in range(sets)])
    target = (t + jnp.arange(n)) % n
    target_begin = jnp.sum(
        jnp.where(target[None, :, None] == jnp.arange(n)[None, None, :], begin[:, None, :], 0), axis=2
    )
    place = (
        target_begin[:, :, None, None] + jnp.arange(piece)[None, None, :, None]
        == jnp.arange(set_rows)[None, None, None, :]
    ).astype(BF)
    own = (order // shard_rows == t)
    mine_rank = jnp.sum(jnp.where((order[None, :] == t * shard_rows + jnp.arange(shard_rows)[:, None]),
                                  jnp.where(alive, rank, -1)[None, :], 0), axis=1)
    spot = jnp.where(mine_rank >= 0, (mine_rank % sets) * piece + mine_rank // sets
                     - jnp.where(mine_rank % sets == 0, target_begin[0, 0], target_begin[1, 0]), -1)
    final = (spot[:, None] == jnp.arange(sets * piece)[None, :]).astype(BF)

    present = all_counts[0] >= 0
    held = after(grad_out, select, present, *token_parts)
    grad_parts = [spread(held, k) for k in range(n)]

    def project(ids, select, gate_weight, up_weight, *token_parts):
        send_far, keep_far, send_near, keep_near = gate_up(ids, select, token_parts, gate_weight, up_weight)
        got_far = lax.ppermute(send_far, "seq", sibling)
        return (keep_far.astype(F32) + got_far.astype(F32)).astype(BF), send_near, keep_near

    def absent(*_):
        nothing = jnp.zeros((2, live_rows, gate_weight.shape[1] // 4), BF)
        return nothing, nothing, nothing

    pair_far, send_near, keep_near = lax.cond(present, project, absent, ids, select, gate_weight, up_weight, *token_parts)
    across_near = lax.ppermute(pair_far, "seq", across)

    outs = hidden_grads(ids, after(select, pair_far), grad_parts, down_weight)
    pairs = []
    for m in range(sets):
        got = lax.ppermute(outs[m], "seq", sibling)
        keep = outs[sets + m]
        pairs.append(((keep[0].astype(F32) + got[0].astype(F32)).astype(BF), keep[1].astype(F32) + got[1].astype(F32)))
    got_near = lax.ppermute(after(send_near, outs[0]), "seq", sibling)
    gate_near = keep_near.astype(F32) + got_near.astype(F32) + across_near.astype(F32)
    ds, ds_core, ds_far = [], [], []
    for m in range(sets):
        pair_far, pair_near = pairs[m]
        got = lax.ppermute(pair_far, "seq", across)
        if m > 0:
            got = after(got, ds[m - 1])
        part = slice(m * set_rows, (m + 1) * set_rows)
        ds.append(jnp.stack(derive(gate_near[0, part], gate_near[1, part], pair_near + got.astype(F32))))
        ds_core.append(lax.ppermute(ds[m], "seq", sibling))
        ds_far.append(lax.ppermute(ds[m], "seq", across))
    firsts = near(ids, ds, ds_core, gate_weight, up_weight)
    pieces, parts = [], firsts
    for m in range(sets):
        d_both = lax.ppermute(after(ds_far[m], parts[0]), "seq", sibling)
        parts = far(ids, place[m].reshape(n * piece, set_rows), ds_far[m], d_both, gate_weight, up_weight, firsts[m])
        total = parts[0].astype(F32)
        for k in range(1, n):
            shift = [(i, (i + k) % n) for i in range(n)]
            total += lax.ppermute(parts[k], "tensor", shift).astype(F32)
        pieces.append(total.astype(BF))
    return jnp.dot(final, jnp.concatenate(pieces), preferred_element_type=F32).astype(BF)


def solution(mesh):
    placed = (
        P(("group", "seq"), "tensor"),
        P(("group", "seq"), "tensor"),
        P(("group", "seq")),
        P("group"),
        P("seq", "tensor"),
        P("seq", "tensor"),
        P("tensor", "seq"),
    )
    if mesh.shape["tensor"] == 4 and mesh.shape["seq"] == 4:
        body = functools.partial(tuned, 4)
    else:
        body = general
    return jax.shard_map(
        body, mesh=mesh, in_specs=placed, out_specs=P(("group", "tensor"), "seq"), check_vma=False
    )
```

```python
import functools
import jax
import jax.numpy as jnp
from jax import lax
from jax.experimental import pallas as pl
from jax.experimental.pallas import tpu as pltpu
from jax.sharding import PartitionSpec as P

BF, F32 = jnp.bfloat16, jnp.float32
ROW_CONTRACT = (((1,), (1,)), ((), ()))
VMEM = 49 * 1024 * 1024
PROJECT_COST, HIDDEN_COST, NEAR_COST, FAR_COST = 20000000, 60000000, 40000000, 40000000


def derive(gate, up, hidden_grad):
    sig = jax.nn.sigmoid(gate)
    d_up = (hidden_grad * gate * sig).astype(BF)
    d_gate = (hidden_grad * up * sig * (1.0 + gate * (1.0 - sig))).astype(BF)
    return (d_gate, d_up)


def general(tokens, grad_out, counts, packing, gate_weight, up_weight, down_weight):
    shard_rows = tokens.shape[0]
    alive_rows = jnp.arange(shard_rows, dtype=jnp.int32) < counts[0]
    masked = jnp.where(alive_rows[:, None], grad_out, jnp.zeros_like(grad_out))
    whole_tokens, whole_cotangent = (
        lax.all_gather(tokens, "tensor", axis=1, tiled=True),
        lax.all_gather(masked, "tensor", axis=1, tiled=True),
    )
    owned_tokens, owned_cotangent = (
        lax.all_to_all(whole_tokens, "seq", split_axis=1, concat_axis=0, tiled=True),
        lax.all_to_all(whole_cotangent, "seq", split_axis=1, concat_axis=0, tiled=True),
    )
    packed_tokens = jnp.take(owned_tokens, packing, axis=0)
    packed_cotangent = jnp.take(owned_cotangent, packing, axis=0)
    gate_part = jnp.dot(packed_tokens, gate_weight, preferred_element_type=F32)
    up_part = jnp.dot(packed_tokens, up_weight, preferred_element_type=F32)
    hidden_part = lax.dot_general(
        packed_cotangent, down_weight, ROW_CONTRACT, preferred_element_type=F32
    )
    gate, up, hidden_grad = (
        lax.psum(gate_part.astype(BF), "seq").astype(F32),
        lax.psum(up_part.astype(BF), "seq").astype(F32),
        lax.psum(hidden_part.astype(BF), "seq").astype(F32),
    )
    d_gate, d_up = derive(gate, up, hidden_grad)
    result = lax.dot_general(d_gate, gate_weight, ROW_CONTRACT, preferred_element_type=F32)
    return lax.psum_scatter(
        (result + lax.dot_general(d_up, up_weight, ROW_CONTRACT, preferred_element_type=F32)).astype(BF),
        "tensor",
        scatter_dimension=0,
        tiled=True,
    )


def region(ref, axis, index, size):
    spot = pl.ds(pl.multiple_of(index * size, size), size)
    return ref.at[spot] if axis == 0 else ref.at[:, spot]


def slot_index(slot, core, x):
    which_core = 1 - core if slot % 2 == 0 else core
    which_x = 1 - x if slot // 2 == 0 else x
    return which_x * 2 + which_core


def start(source, target, sem):
    copy = pltpu.make_async_copy(source, target, sem)
    copy.start()
    return copy


class Stream:
    def __init__(self, copies, ahead):
        self.copies, self.ahead, self.begun = copies, ahead, 0
        self.reach(0)

    def reach(self, index):
        while self.begun < min(index + self.ahead, len(self.copies)):
            for copy in self.copies[self.begun]:
                copy.start()
            self.begun += 1

    def wait(self, index):
        for copy in self.copies[index]:
            copy.wait()
        self.reach(index + 1)


IN_VMEM = pl.BlockSpec(memory_space=pltpu.VMEM)
IN_HBM = pl.BlockSpec(memory_space=pl.ANY)
IN_SMEM = pl.BlockSpec(memory_space=pltpu.SMEM)


def call(kernel, in_specs, out_shape, scratch, cost):
    return pl.pallas_call(
        kernel,
        in_specs=in_specs,
        out_specs=[IN_HBM] * len(out_shape),
        out_shape=[jax.ShapeDtypeStruct(shape, dtype) for shape, dtype in out_shape],
        scratch_shapes=scratch,
        compiler_params=pltpu.CompilerParams(vmem_limit_bytes=VMEM),
        cost_estimate=pl.CostEstimate(flops=0, bytes_accessed=cost, transcendentals=0),
    )


def pick_start(parts, arrived, sems):
    width = parts[0].shape[0]
    return [start(part, arrived.at[pl.ds(k * width, width)], sems.at[k]) for k, part in enumerate(parts)]


def pick_end(moves, select_ref, arrived, rows_v):
    for move in moves:
        move.wait()
    rows_v[...] = jnp.dot(select_ref[...], arrived[...], preferred_element_type=F32).astype(BF)


def project_kernel(near, ids, *refs):
    if near:
        rows_in, gate_w, up_w, send, keep, gate_v, up_v, out_v, rows_v, sems = refs
        moves = [start(rows_in, rows_v, sems.at[0, 0])]
    else:
        select_ref, p0, p1, p2, p3, gate_w, up_w, send, keep, rows_out, gate_v, up_v, out_v, rows_v, arrived, sems = refs
        moves = pick_start((p0, p1, p2, p3), arrived, sems.at[0])
    core, x = ids[0], ids[1]
    block = gate_v.shape[2]
    loads = []
    for i in range(2):
        index = slot_index(2 * near + i, core, x)
        for a, (weight, held) in enumerate(((gate_w, gate_v), (up_w, up_v))):
            loads.append([pltpu.make_async_copy(region(weight, 1, index, block), held.at[i], sems.at[1 + a, i])])
    loads = Stream(loads, 2)
    stores = []
    if near:
        moves[0].wait()
    else:
        pick_end(moves, select_ref, arrived, rows_v)
        stores.append(start(rows_v, rows_out, sems.at[0, 0]))
    for i, out in enumerate((send, keep)):
        for a, held in enumerate((gate_v, up_v)):
            loads.wait(2 * i + a)
            out_v[i, a] = jnp.dot(rows_v[...], held[i], preferred_element_type=F32).astype(BF)
            stores.append(start(out_v.at[i, a], out.at[a], sems.at[3 + a, i]))
    for store in stores:
        store.wait()


def project(near, ids, rows, gate_weight, up_weight):
    depth, block = gate_weight.shape[0], gate_weight.shape[1] // 4
    count = rows.shape[0] if near else rows[0].shape[0]
    args = (rows,) if near else rows
    picked = [] if near else [((count, depth), BF)]
    arrived = [] if near else [pltpu.VMEM((rows[0].shape[1], depth), BF)]
    return call(
        functools.partial(project_kernel, near),
        [IN_SMEM] + [IN_HBM if near else IN_VMEM] + [IN_HBM] * (len(args) + 1),
        [((2, count, block), BF)] * 2 + picked,
        [pltpu.VMEM((2, depth, block), BF)] * 2 + [
            pltpu.VMEM((2, 2, count, block), BF),
            pltpu.VMEM((count, depth), BF),
        ] + arrived + [pltpu.SemaphoreType.DMA((5, 4))],
        PROJECT_COST,
    )(ids, *args, gate_weight, up_weight)


def hidden_kernel(near, ids, *refs):
    if near:
        rows_in, down, send, keep, down_v, out_v, rows_v, sems = refs
        moves = [start(rows_in, rows_v, sems.at[0, 0])]
        outs = ((send,), (keep,))
    else:
        select_ref, p0, p1, p2, p3, down, *sides, rows_out, down_v, out_v, rows_v, arrived, sems = refs
        moves = pick_start((p0, p1, p2, p3), arrived, sems.at[0])
        outs = (sides[:2], sides[2:])
    core, x = ids[0], ids[1]
    block = down_v.shape[1]
    loads = Stream(
        [[pltpu.make_async_copy(region(down, 0, slot_index(2 * near + i, core, x), block), down_v.at[i], sems.at[1, i])]
         for i in range(2)], 2)
    stores = []
    if near:
        moves[0].wait()
    else:
        pick_end(moves, select_ref, arrived, rows_v)
        stores.append(start(rows_v, rows_out, sems.at[0, 0]))
    for i in range(2):
        loads.wait(i)
        hidden = lax.dot_general(rows_v[...], down_v[i], ROW_CONTRACT, preferred_element_type=F32)
        out_v[i] = hidden.astype(BF)
        for m, out in enumerate(outs[i]):
            rows = out.shape[0]
            stores.append(start(out_v.at[i, pl.ds(m * rows, rows)], out, sems.at[2 + m, i]))
    for store in stores:
        store.wait()


def hidden_grads(near, ids, rows, down_weight):
    depth, block = down_weight.shape[1], down_weight.shape[0] // 4
    count = rows.shape[0] if near else rows[0].shape[0]
    args = (rows,) if near else rows
    outs = [((count, block), BF)] * 2 if near else [((count // 2, block), BF)] * 4 + [((count, depth), BF)]
    arrived = [] if near else [pltpu.VMEM((rows[0].shape[1], depth), BF)]
    return call(
        functools.partial(hidden_kernel, near),
        [IN_SMEM] + [IN_HBM if near else IN_VMEM] + [IN_HBM] * len(args),
        outs,
        [
            pltpu.VMEM((2, block, depth), BF),
            pltpu.VMEM((2, count, block), BF),
            pltpu.VMEM((count, depth), BF),
        ] + arrived + [pltpu.SemaphoreType.DMA((4, 4))],
        HIDDEN_COST,
    )(ids, *args, down_weight)


CHUNKS = 4


def back_begin(core, which_x, pairs, gate_w, up_w, grads_v, weight_v, sems, grad_sems):
    rows, block = pairs[0][0].shape[1], pairs[0][0].shape[2]
    height, width = gate_w.shape[0] // CHUNKS, 2 * block
    moves = []
    for m, pair in enumerate(pairs):
        for source, value in enumerate(pair):
            which_core = core if source == 0 else 1 - core
            spot = pl.ds(pl.multiple_of(which_core * block, block), block)
            for a in range(2):
                moves.append(start(value.at[a], grads_v.at[a, pl.ds(m * rows, rows), spot],
                                   grad_sems.at[m, 2 * source + a]))
    side = pl.ds(pl.multiple_of(which_x * width, width), width)
    loads = []
    for chunk in range(CHUNKS):
        high = pl.ds(chunk * height, height)
        loads.append([
            pltpu.make_async_copy(weight.at[high, side], weight_v.at[a, high], sems.at[chunk, a])
            for a, weight in enumerate((gate_w, up_w))
        ])
    return moves, Stream(loads, 2)


def back_chunk(chunk, grads_v, weight_v, loads):
    height = weight_v.shape[1] // CHUNKS
    spot = pl.ds(chunk * height, height)
    loads.wait(chunk)
    total = lax.dot_general(grads_v[0], weight_v[0, spot], ROW_CONTRACT, preferred_element_type=F32)
    return total + lax.dot_general(grads_v[1], weight_v[1, spot], ROW_CONTRACT, preferred_element_type=F32)


def near_kernel(ids, mine_a, other_a, mine_b, other_b, gate_w, up_w, out_a, out_b,
                grads_v, weight_v, out_v, sems, grad_sems, out_sems):
    moves, loads = back_begin(ids[0], ids[1], ((mine_a, other_a), (mine_b, other_b)), gate_w, up_w,
                              grads_v, weight_v, sems, grad_sems)
    height, rows = gate_w.shape[0] // CHUNKS, out_a.shape[0]
    for move in moves:
        move.wait()
    stores = []
    for chunk in range(CHUNKS):
        spot = pl.ds(chunk * height, height)
        out_v[:, spot] = back_chunk(chunk, grads_v, weight_v, loads)
        for m, out in enumerate((out_a, out_b)):
            stores.append(start(out_v.at[pl.ds(m * rows, rows), spot], out.at[:, spot], out_sems.at[chunk, m]))
    for store in stores:
        store.wait()


def far_kernel(ids, place_ref, mine, other, gate_w, up_w, first, o0, o1, o2, o3,
               grads_v, weight_v, first_v, out_v, sems, grad_sems, out_sems, first_sem):
    begun = start(first, first_v, first_sem.at[0])
    moves, loads = back_begin(ids[0], 1 - ids[1], ((mine, other),), gate_w, up_w, grads_v, weight_v, sems, grad_sems)
    height = gate_w.shape[0] // CHUNKS
    piece = o0.shape[0]
    for move in [begun] + moves:
        move.wait()
    stores = []
    for chunk in range(CHUNKS):
        spot = pl.ds(chunk * height, height)
        total = first_v[:, spot] + back_chunk(chunk, grads_v, weight_v, loads)
        out_v[:, spot] = jnp.dot(place_ref[...], total.astype(BF), preferred_element_type=F32).astype(BF)
        for k, out in enumerate((o0, o1, o2, o3)):
            part = out_v.at[pl.ds(k * piece, piece), spot]
            stores.append(start(part, out.at[:, spot], out_sems.at[chunk, k]))
    for store in stores:
        store.wait()


def near_back(ids, mine, other, gate_weight, up_weight):
    sets, rows, block, depth = len(mine), mine[0].shape[1], mine[0].shape[2], gate_weight.shape[0]
    count = sets * rows
    return call(
        near_kernel,
        [IN_SMEM] + [IN_HBM] * 6,
        [((rows, depth), F32)] * 2,
        [
            pltpu.VMEM((2, count, 2 * block), BF),
            pltpu.VMEM((2, depth, 2 * block), BF),
            pltpu.VMEM((count, depth), F32),
            pltpu.SemaphoreType.DMA((CHUNKS, 2)),
            pltpu.SemaphoreType.DMA((sets, 4)),
            pltpu.SemaphoreType.DMA((CHUNKS, sets)),
        ],
        NEAR_COST,
    )(ids, mine[0], other[0], mine[1], other[1], gate_weight, up_weight)


def far_back(ids, place, mine, other, gate_weight, up_weight, first):
    rows, block, depth = mine.shape[1], mine.shape[2], gate_weight.shape[0]
    count = place.shape[0]
    return call(
        far_kernel,
        [IN_SMEM, IN_VMEM] + [IN_HBM] * 5,
        [((count // 4, depth), BF)] * 4,
        [
            pltpu.VMEM((2, rows, 2 * block), BF),
            pltpu.VMEM((2, depth, 2 * block), BF),
            pltpu.VMEM((rows, depth), F32),
            pltpu.VMEM((count, depth), BF),
            pltpu.SemaphoreType.DMA((CHUNKS, 2)),
            pltpu.SemaphoreType.DMA((1, 4)),
            pltpu.SemaphoreType.DMA((CHUNKS, 4)),
            pltpu.SemaphoreType.DMA((1,)),
        ],
        FAR_COST,
    )(ids, place, mine, other, gate_weight, up_weight, first)


def after(value, *others):
    return lax.optimization_barrier((value,) + others)[0]


def tuned(n, tokens, grad_out, counts, packing, gate_weight, up_weight, down_weight):
    shard_rows, depth = tokens.shape
    rows = packing.shape[0]
    live_rows = rows * 3 // 4
    sets, block = 2, gate_weight.shape[1] // 4
    set_rows, piece = live_rows // sets, shard_rows // sets
    t, s = lax.axis_index("tensor"), lax.axis_index("seq")
    core, x = s % 2, s // 2
    ids = jnp.stack([core, x]).astype(jnp.int32)
    sibling = [(i, i ^ 1) for i in range(n)]
    across = [(i, i ^ 2) for i in range(n)]

    def spread(value, k):
        pairs = [(a * n + b, ((b + k) % n) * n + a) for a in range(n) for b in range(n)]
        return lax.ppermute(value, ("tensor", "seq"), pairs)

    token_parts = [spread(tokens, k) for k in range(n)]

    all_counts = lax.all_gather(counts, "seq", tiled=True)
    home, place_in = packing // shard_rows, packing % shard_rows
    bound = jnp.sum(jnp.where(home[:, None] == jnp.arange(n)[None, :], all_counts[None, :], 0), axis=1)
    alive = place_in < bound
    order = jnp.arange(rows, dtype=jnp.int32)
    rank = jnp.sum(jnp.where(order[None, :] < order[:, None], alive[None, :].astype(jnp.int32), 0), axis=1)
    index = jnp.where(alive, (rank % sets) * set_rows + rank // sets, -1)
    slot = jnp.arange(rows, dtype=jnp.int32)
    arriving = ((t - slot // shard_rows) % n) * shard_rows + slot % shard_rows
    to_row = (index[None, :] == jnp.arange(live_rows, dtype=jnp.int32)[:, None]).astype(BF)
    from_slot = (packing[:, None] == arriving[None, :]).astype(BF)
    select = jnp.dot(to_row, from_slot, preferred_element_type=F32).astype(BF)
    before = jnp.sum(
        jnp.where(order[None, :] < (jnp.arange(n) * shard_rows)[:, None], alive[None, :].astype(jnp.int32), 0), axis=1
    )
    begin = jnp.stack([(before + sets - 1 - m) // sets for m in range(sets)])
    target = (t + jnp.arange(n)) % n
    target_begin = jnp.sum(
        jnp.where(target[None, :, None] == jnp.arange(n)[None, None, :], begin[:, None, :], 0), axis=2
    )
    place = (
        target_begin[:, :, None, None] + jnp.arange(piece)[None, None, :, None]
        == jnp.arange(set_rows)[None, None, None, :]
    ).astype(BF)
    own = (order // shard_rows == t)
    mine_rank = jnp.sum(jnp.where((order[None, :] == t * shard_rows + jnp.arange(shard_rows)[:, None]),
                                  jnp.where(alive, rank, -1)[None, :], 0), axis=1)
    spot = jnp.where(mine_rank >= 0, (mine_rank % sets) * piece + mine_rank // sets
                     - jnp.where(mine_rank % sets == 0, target_begin[0, 0], target_begin[1, 0]), -1)
    final = (spot[:, None] == jnp.arange(sets * piece)[None, :]).astype(BF)

    present = all_counts[0] >= 0
    held = after(grad_out, select, present, *token_parts)
    grad_parts = [spread(held, k) for k in range(n)]

    def far_side(ids, select, gate_weight, up_weight, *token_parts):
        send, keep, picked = project(False, ids, (select, *token_parts), gate_weight, up_weight)
        got = lax.ppermute(send, "seq", sibling)
        return (keep.astype(F32) + got.astype(F32)).astype(BF), picked

    def absent(*_):
        return jnp.zeros((2, live_rows, block), BF), jnp.zeros((live_rows, depth), BF)

    pair_far, picked = lax.cond(present, far_side, absent, ids, select, gate_weight, up_weight, *token_parts)
    across_near = lax.ppermute(pair_far, "seq", across)

    send, keep = project(True, ids, picked, gate_weight, up_weight)
    *outs, picked = hidden_grads(False, ids, (after(select, send), *grad_parts), down_weight)
    near = keep.astype(F32) + lax.ppermute(after(send, outs[0]), "seq", sibling).astype(F32) + across_near.astype(F32)
    pairs = []
    for m in range(sets):
        got = lax.ppermute(outs[m], "seq", sibling)
        keep = after(outs[sets + m], pairs[0]) if m else outs[sets]
        pairs.append((keep.astype(F32) + got.astype(F32)).astype(BF))
    def near_side(ids, picked, down_weight):
        send, keep = hidden_grads(True, ids, picked, down_weight)
        return keep, lax.ppermute(send, "seq", sibling)

    def no_near(*_):
        return (jnp.zeros((live_rows, block), BF),) * 2

    keep, got = lax.cond(present, near_side, no_near, after(ids, pairs[-1]), picked, down_weight)
    hidden = keep.astype(F32) + got.astype(F32)
    ds, ds_core, ds_far = [], [], []
    for m in range(sets):
        got = lax.ppermute(pairs[m], "seq", across)
        if m > 0:
            got = after(got, ds[m - 1])
        part = slice(m * set_rows, (m + 1) * set_rows)
        ds.append(jnp.stack(derive(near[0, part], near[1, part], hidden[part] + got.astype(F32))))
        ds_core.append(lax.ppermute(ds[m], "seq", sibling))
        ds_far.append(lax.ppermute(ds[m], "seq", across))
    firsts = near_back(ids, ds, ds_core, gate_weight, up_weight)
    pieces, parts = [], firsts
    for m in range(sets):
        d_both = lax.ppermute(after(ds_far[m], parts[0]), "seq", sibling)
        parts = far_back(ids, place[m].reshape(n * piece, set_rows), ds_far[m], d_both, gate_weight, up_weight, firsts[m])
        total = parts[0].astype(F32)
        for k in range(1, n):
            shift = [(i, (i + k) % n) for i in range(n)]
            total += lax.ppermute(parts[k], "tensor", shift).astype(F32)
        pieces.append(total.astype(BF))
    return jnp.dot(final, jnp.concatenate(pieces), preferred_element_type=F32).astype(BF)


def solution(mesh):
    placed = (
        P(("group", "seq"), "tensor"),
        P(("group", "seq"), "tensor"),
        P(("group", "seq")),
        P("group"),
        P("seq", "tensor"),
        P("seq", "tensor"),
        P("tensor", "seq"),
    )
    if mesh.shape["tensor"] == 4 and mesh.shape["seq"] == 4:
        body = functools.partial(tuned, 4)
    else:
        body = general
    return jax.shard_map(
        body, mesh=mesh, in_specs=placed, out_specs=P(("group", "tensor"), "seq"), check_vma=False
    )
```

```python
import functools
import jax
import jax.numpy as jnp
from jax import lax
from jax.experimental import pallas as pl
from jax.experimental.pallas import tpu as pltpu
from jax.sharding import PartitionSpec as P

BF, F32 = jnp.bfloat16, jnp.float32
ROW_CONTRACT = (((1,), (1,)), ((), ()))
VMEM = 49 * 1024 * 1024
PROJECT_COST, HIDDEN_COST, NEAR_COST, FAR_COST = 20000000, 60000000, 40000000, 40000000


def derive(gate, up, hidden_grad):
    sig = jax.nn.sigmoid(gate)
    d_up = (hidden_grad * gate * sig).astype(BF)
    d_gate = (hidden_grad * up * sig * (1.0 + gate * (1.0 - sig))).astype(BF)
    return (d_gate, d_up)


def general(tokens, grad_out, counts, packing, gate_weight, up_weight, down_weight):
    shard_rows = tokens.shape[0]
    alive_rows = jnp.arange(shard_rows, dtype=jnp.int32) < counts[0]
    masked = jnp.where(alive_rows[:, None], grad_out, jnp.zeros_like(grad_out))
    whole_tokens, whole_cotangent = (
        lax.all_gather(tokens, "tensor", axis=1, tiled=True),
        lax.all_gather(masked, "tensor", axis=1, tiled=True),
    )
    owned_tokens, owned_cotangent = (
        lax.all_to_all(whole_tokens, "seq", split_axis=1, concat_axis=0, tiled=True),
        lax.all_to_all(whole_cotangent, "seq", split_axis=1, concat_axis=0, tiled=True),
    )
    packed_tokens = jnp.take(owned_tokens, packing, axis=0)
    packed_cotangent = jnp.take(owned_cotangent, packing, axis=0)
    gate_part = jnp.dot(packed_tokens, gate_weight, preferred_element_type=F32)
    up_part = jnp.dot(packed_tokens, up_weight, preferred_element_type=F32)
    hidden_part = lax.dot_general(
        packed_cotangent, down_weight, ROW_CONTRACT, preferred_element_type=F32
    )
    gate, up, hidden_grad = (
        lax.psum(gate_part.astype(BF), "seq").astype(F32),
        lax.psum(up_part.astype(BF), "seq").astype(F32),
        lax.psum(hidden_part.astype(BF), "seq").astype(F32),
    )
    d_gate, d_up = derive(gate, up, hidden_grad)
    result = lax.dot_general(d_gate, gate_weight, ROW_CONTRACT, preferred_element_type=F32)
    return lax.psum_scatter(
        (result + lax.dot_general(d_up, up_weight, ROW_CONTRACT, preferred_element_type=F32)).astype(BF),
        "tensor",
        scatter_dimension=0,
        tiled=True,
    )


def region(ref, axis, index, size):
    spot = pl.ds(pl.multiple_of(index * size, size), size)
    return ref.at[spot] if axis == 0 else ref.at[:, spot]


def slot_index(slot, core, x):
    which_core = 1 - core if slot % 2 == 0 else core
    which_x = 1 - x if slot // 2 == 0 else x
    return which_x * 2 + which_core


def start(source, target, sem):
    copy = pltpu.make_async_copy(source, target, sem)
    copy.start()
    return copy


class Stream:
    def __init__(self, copies, ahead):
        self.copies, self.ahead, self.begun = copies, ahead, 0
        self.reach(0)

    def reach(self, index):
        while self.begun < min(index + self.ahead, len(self.copies)):
            for copy in self.copies[self.begun]:
                copy.start()
            self.begun += 1

    def wait(self, index):
        for copy in self.copies[index]:
            copy.wait()
        self.reach(index + 1)


IN_VMEM = pl.BlockSpec(memory_space=pltpu.VMEM)
IN_HBM = pl.BlockSpec(memory_space=pl.ANY)
IN_SMEM = pl.BlockSpec(memory_space=pltpu.SMEM)


def call(kernel, in_specs, out_shape, scratch, cost):
    return pl.pallas_call(
        kernel,
        in_specs=in_specs,
        out_specs=[IN_HBM] * len(out_shape),
        out_shape=[jax.ShapeDtypeStruct(shape, dtype) for shape, dtype in out_shape],
        scratch_shapes=scratch,
        compiler_params=pltpu.CompilerParams(vmem_limit_bytes=VMEM),
        cost_estimate=pl.CostEstimate(flops=0, bytes_accessed=cost, transcendentals=0),
    )


def pick_start(parts, arrived, sems):
    width = parts[0].shape[0]
    return [start(part, arrived.at[pl.ds(k * width, width)], sems.at[k]) for k, part in enumerate(parts)]


def pick_end(moves, select_ref, arrived, rows_v):
    for move in moves:
        move.wait()
    rows_v[...] = jnp.dot(select_ref[...], arrived[...], preferred_element_type=F32).astype(BF)


def project_kernel(near, ids, *refs):
    if near:
        rows_in, gate_w, up_w, send, keep, gate_v, up_v, out_v, rows_v, sems = refs
        moves = [start(rows_in, rows_v, sems.at[0, 0])]
    else:
        select_ref, p0, p1, p2, p3, gate_w, up_w, send, keep, rows_out, gate_v, up_v, out_v, rows_v, arrived, sems = refs
        moves = pick_start((p0, p1, p2, p3), arrived, sems.at[0])
    core, x = ids[0], ids[1]
    block = gate_v.shape[2]
    loads = []
    for i in range(2):
        index = slot_index(2 * near + i, core, x)
        for a, (weight, held) in enumerate(((gate_w, gate_v), (up_w, up_v))):
            loads.append([pltpu.make_async_copy(region(weight, 1, index, block), held.at[i], sems.at[1 + a, i])])
    loads = Stream(loads, 2)
    stores = []
    if near:
        moves[0].wait()
    else:
        pick_end(moves, select_ref, arrived, rows_v)
        stores.append(start(rows_v, rows_out, sems.at[0, 0]))
    for i, out in enumerate((send, keep)):
        for a, held in enumerate((gate_v, up_v)):
            loads.wait(2 * i + a)
            out_v[i, a] = jnp.dot(rows_v[...], held[i], preferred_element_type=F32).astype(BF)
            stores.append(start(out_v.at[i, a], out.at[a], sems.at[3 + a, i]))
    for store in stores:
        store.wait()


def project(near, ids, rows, gate_weight, up_weight):
    depth, block = gate_weight.shape[0], gate_weight.shape[1] // 4
    count = rows.shape[0] if near else rows[0].shape[0]
    args = (rows,) if near else rows
    picked = [] if near else [((count, depth), BF)]
    arrived = [] if near else [pltpu.VMEM((rows[0].shape[1], depth), BF)]
    return call(
        functools.partial(project_kernel, near),
        [IN_SMEM] + [IN_HBM if near else IN_VMEM] + [IN_HBM] * (len(args) + 1),
        [((2, count, block), BF)] * 2 + picked,
        [pltpu.VMEM((2, depth, block), BF)] * 2 + [
            pltpu.VMEM((2, 2, count, block), BF),
            pltpu.VMEM((count, depth), BF),
        ] + arrived + [pltpu.SemaphoreType.DMA((5, 4))],
        PROJECT_COST,
    )(ids, *args, gate_weight, up_weight)


def hidden_kernel(near, ids, *refs):
    if near:
        rows_in, down, send, keep, down_v, out_v, rows_v, sems = refs
        moves = [start(rows_in, rows_v, sems.at[0, 0])]
        outs = ((send,), (keep,))
    else:
        order_ref, *parts, down, o0, o1, o2, o3, rows_out, down_v, out_v, rows_v, sems = refs
        outs = ((o0, o1), (o2, o3))
    core, x = ids[0], ids[1]
    block = down_v.shape[1]
    loads = Stream(
        [[pltpu.make_async_copy(region(down, 0, slot_index(2 * near + i, core, x), block), down_v.at[i], sems.at[1, i])]
         for i in range(2)], 2)
    stores = []
    if near:
        moves[0].wait()
    else:
        total = jnp.dot(order_ref[0], parts[0][...], preferred_element_type=F32)
        for k in range(1, len(parts)):
            total += jnp.dot(order_ref[k], parts[k][...], preferred_element_type=F32)
        rows_v[...] = total.astype(BF)
        stores.append(start(rows_v, rows_out, sems.at[0, 0]))
    for i in range(2):
        loads.wait(i)
        hidden = lax.dot_general(rows_v[...], down_v[i], ROW_CONTRACT, preferred_element_type=F32)
        out_v[i] = hidden.astype(BF)
        for m, out in enumerate(outs[i]):
            rows = out.shape[0]
            stores.append(start(out_v.at[i, pl.ds(m * rows, rows)], out, sems.at[2 + m, i]))
    for store in stores:
        store.wait()


def hidden_grads(near, ids, rows, down_weight):
    depth, block = down_weight.shape[1], down_weight.shape[0] // 4
    count = rows.shape[0] if near else rows[0].shape[1]
    args = (rows,) if near else rows
    outs = [((count, block), BF)] * 2 if near else [((count // 2, block), BF)] * 4 + [((count, depth), BF)]
    return call(
        functools.partial(hidden_kernel, near),
        [IN_SMEM] + [IN_HBM if near else IN_VMEM] * len(args) + [IN_HBM],
        outs,
        [
            pltpu.VMEM((2, block, depth), BF),
            pltpu.VMEM((2, count, block), BF),
            pltpu.VMEM((count, depth), BF),
            pltpu.SemaphoreType.DMA((4, 4)),
        ],
        HIDDEN_COST,
    )(ids, *args, down_weight)


CHUNKS = 4


def back_begin(core, which_x, pairs, gate_w, up_w, grads_v, weight_v, sems, grad_sems):
    rows, block = pairs[0][0].shape[1], pairs[0][0].shape[2]
    height, width = gate_w.shape[0] // CHUNKS, 2 * block
    moves = []
    for m, pair in enumerate(pairs):
        for source, value in enumerate(pair):
            which_core = core if source == 0 else 1 - core
            spot = pl.ds(pl.multiple_of(which_core * block, block), block)
            for a in range(2):
                moves.append(start(value.at[a], grads_v.at[a, pl.ds(m * rows, rows), spot],
                                   grad_sems.at[m, 2 * source + a]))
    side = pl.ds(pl.multiple_of(which_x * width, width), width)
    loads = []
    for chunk in range(CHUNKS):
        high = pl.ds(chunk * height, height)
        loads.append([
            pltpu.make_async_copy(weight.at[high, side], weight_v.at[a, high], sems.at[chunk, a])
            for a, weight in enumerate((gate_w, up_w))
        ])
    return moves, Stream(loads, 2)


def back_chunk(chunk, grads_v, weight_v, loads):
    height = weight_v.shape[1] // CHUNKS
    spot = pl.ds(chunk * height, height)
    loads.wait(chunk)
    total = lax.dot_general(grads_v[0], weight_v[0, spot], ROW_CONTRACT, preferred_element_type=F32)
    return total + lax.dot_general(grads_v[1], weight_v[1, spot], ROW_CONTRACT, preferred_element_type=F32)


def near_kernel(ids, mine_a, other_a, mine_b, other_b, gate_w, up_w, out_a, out_b,
                grads_v, weight_v, out_v, sems, grad_sems, out_sems):
    moves, loads = back_begin(ids[0], ids[1], ((mine_a, other_a), (mine_b, other_b)), gate_w, up_w,
                              grads_v, weight_v, sems, grad_sems)
    height, rows = gate_w.shape[0] // CHUNKS, out_a.shape[0]
    for move in moves:
        move.wait()
    stores = []
    for chunk in range(CHUNKS):
        spot = pl.ds(chunk * height, height)
        out_v[:, spot] = back_chunk(chunk, grads_v, weight_v, loads)
        for m, out in enumerate((out_a, out_b)):
            stores.append(start(out_v.at[pl.ds(m * rows, rows), spot], out.at[:, spot], out_sems.at[chunk, m]))
    for store in stores:
        store.wait()


def far_kernel(ids, place_ref, mine, other, gate_w, up_w, first, o0, o1, o2, o3,
               grads_v, weight_v, first_v, out_v, sems, grad_sems, out_sems, first_sem):
    begun = start(first, first_v, first_sem.at[0])
    moves, loads = back_begin(ids[0], 1 - ids[1], ((mine, other),), gate_w, up_w, grads_v, weight_v, sems, grad_sems)
    height = gate_w.shape[0] // CHUNKS
    piece = o0.shape[0]
    for move in [begun] + moves:
        move.wait()
    stores = []
    for chunk in range(CHUNKS):
        spot = pl.ds(chunk * height, height)
        total = first_v[:, spot] + back_chunk(chunk, grads_v, weight_v, loads)
        out_v[:, spot] = jnp.dot(place_ref[...], total.astype(BF), preferred_element_type=F32).astype(BF)
        for k, out in enumerate((o0, o1, o2, o3)):
            part = out_v.at[pl.ds(k * piece, piece), spot]
            stores.append(start(part, out.at[:, spot], out_sems.at[chunk, k]))
    for store in stores:
        store.wait()


def near_back(ids, mine, other, gate_weight, up_weight):
    sets, rows, block, depth = len(mine), mine[0].shape[1], mine[0].shape[2], gate_weight.shape[0]
    count = sets * rows
    return call(
        near_kernel,
        [IN_SMEM] + [IN_HBM] * 6,
        [((rows, depth), F32)] * 2,
        [
            pltpu.VMEM((2, count, 2 * block), BF),
            pltpu.VMEM((2, depth, 2 * block), BF),
            pltpu.VMEM((count, depth), F32),
            pltpu.SemaphoreType.DMA((CHUNKS, 2)),
            pltpu.SemaphoreType.DMA((sets, 4)),
            pltpu.SemaphoreType.DMA((CHUNKS, sets)),
        ],
        NEAR_COST,
    )(ids, mine[0], other[0], mine[1], other[1], gate_weight, up_weight)


def far_back(ids, place, mine, other, gate_weight, up_weight, first):
    rows, block, depth = mine.shape[1], mine.shape[2], gate_weight.shape[0]
    count = place.shape[0]
    return call(
        far_kernel,
        [IN_SMEM, IN_VMEM] + [IN_HBM] * 5,
        [((count // 4, depth), BF)] * 4,
        [
            pltpu.VMEM((2, rows, 2 * block), BF),
            pltpu.VMEM((2, depth, 2 * block), BF),
            pltpu.VMEM((rows, depth), F32),
            pltpu.VMEM((count, depth), BF),
            pltpu.SemaphoreType.DMA((CHUNKS, 2)),
            pltpu.SemaphoreType.DMA((1, 4)),
            pltpu.SemaphoreType.DMA((CHUNKS, 4)),
            pltpu.SemaphoreType.DMA((1,)),
        ],
        FAR_COST,
    )(ids, place, mine, other, gate_weight, up_weight, first)


def after(value, *others):
    return lax.optimization_barrier((value,) + others)[0]


def tuned(n, tokens, grad_out, counts, packing, gate_weight, up_weight, down_weight):
    shard_rows, depth = tokens.shape
    rows = packing.shape[0]
    live_rows = rows * 3 // 4
    sets, block = 2, gate_weight.shape[1] // 4
    set_rows, piece = live_rows // sets, shard_rows // sets
    t, s = lax.axis_index("tensor"), lax.axis_index("seq")
    core, x = s % 2, s // 2
    ids = jnp.stack([core, x]).astype(jnp.int32)
    sibling = [(i, i ^ 1) for i in range(n)]
    across = [(i, i ^ 2) for i in range(n)]

    def spread(value, k):
        pairs = [(a * n + b, ((b + k) % n) * n + a) for a in range(n) for b in range(n)]
        return lax.ppermute(value, ("tensor", "seq"), pairs)

    token_parts = [spread(tokens, k) for k in range(n)]

    all_counts = lax.all_gather(counts, "seq", tiled=True)
    home, place_in = packing // shard_rows, packing % shard_rows
    bound = jnp.sum(jnp.where(home[:, None] == jnp.arange(n)[None, :], all_counts[None, :], 0), axis=1)
    alive = place_in < bound
    order = jnp.arange(rows, dtype=jnp.int32)
    rank = jnp.sum(jnp.where(order[None, :] < order[:, None], alive[None, :].astype(jnp.int32), 0), axis=1)
    index = jnp.where(alive, (rank % sets) * set_rows + rank // sets, -1)
    slot = jnp.arange(rows, dtype=jnp.int32)
    arriving = ((t - slot // shard_rows) % n) * shard_rows + slot % shard_rows
    to_row = (index[None, :] == jnp.arange(live_rows, dtype=jnp.int32)[:, None]).astype(BF)
    from_slot = (packing[:, None] == arriving[None, :]).astype(BF)
    select = jnp.dot(to_row, from_slot, preferred_element_type=F32).astype(BF)
    before = jnp.sum(
        jnp.where(order[None, :] < (jnp.arange(n) * shard_rows)[:, None], alive[None, :].astype(jnp.int32), 0), axis=1
    )
    begin = jnp.stack([(before + sets - 1 - m) // sets for m in range(sets)])
    target = (t + jnp.arange(n)) % n
    target_begin = jnp.sum(
        jnp.where(target[None, :, None] == jnp.arange(n)[None, None, :], begin[:, None, :], 0), axis=2
    )
    place = (
        target_begin[:, :, None, None] + jnp.arange(piece)[None, None, :, None]
        == jnp.arange(set_rows)[None, None, None, :]
    ).astype(BF)
    own = (order // shard_rows == t)
    mine_rank = jnp.sum(jnp.where((order[None, :] == t * shard_rows + jnp.arange(shard_rows)[:, None]),
                                  jnp.where(alive, rank, -1)[None, :], 0), axis=1)
    spot = jnp.where(mine_rank >= 0, (mine_rank % sets) * piece + mine_rank // sets
                     - jnp.where(mine_rank % sets == 0, target_begin[0, 0], target_begin[1, 0]), -1)
    final = (spot[:, None] == jnp.arange(sets * piece)[None, :]).astype(BF)

    present = all_counts[0] >= 0

    share = live_rows // n
    shards = jnp.stack([s, s ^ 2, s ^ 1, s ^ 3])
    to_share = (index[None, :] == share * s + jnp.arange(share, dtype=jnp.int32)[:, None]).astype(BF)
    local = shards[slot // shard_rows] * shard_rows + slot % shard_rows
    from_local = (packing[:, None] == local[None, :]).astype(BF)
    pick = jnp.dot(to_share, from_local, preferred_element_type=F32).astype(BF)
    came = (t - jnp.arange(n, dtype=jnp.int32)) % n
    order_of = (
        jnp.arange(live_rows, dtype=jnp.int32)[None, :, None]
        == (share * came[:, None] + jnp.arange(share, dtype=jnp.int32)[None, :])[:, None, :]
    ).astype(BF)

    def balance(grad_out, far, pick):
        mine = jnp.concatenate([grad_out, far])
        whole = jnp.concatenate([mine, lax.ppermute(mine, "seq", sibling)])
        return jnp.dot(pick, whole, preferred_element_type=F32).astype(BF)

    def no_balance(*_):
        return jnp.zeros((share, depth), BF)

    held = lax.cond(present, balance, no_balance, grad_out, lax.ppermute(grad_out, "seq", across), pick)
    held = after(held, select, present, order_of, *token_parts)
    grad_parts = [spread(held, k) for k in range(n)]

    def far_side(ids, select, gate_weight, up_weight, *token_parts):
        send, keep, picked = project(False, ids, (select, *token_parts), gate_weight, up_weight)
        got = lax.ppermute(send, "seq", sibling)
        return (keep.astype(F32) + got.astype(F32)).astype(BF), picked

    def absent(*_):
        return jnp.zeros((2, live_rows, block), BF), jnp.zeros((live_rows, depth), BF)

    pair_far, picked = lax.cond(present, far_side, absent, ids, select, gate_weight, up_weight, *token_parts)
    across_near = lax.ppermute(pair_far, "seq", across)

    send, keep = project(True, ids, picked, gate_weight, up_weight)
    *outs, picked = hidden_grads(False, ids, (after(order_of, send), *grad_parts), down_weight)
    near = keep.astype(F32) + lax.ppermute(after(send, outs[0]), "seq", sibling).astype(F32) + across_near.astype(F32)
    pairs = []
    for m in range(sets):
        got = lax.ppermute(outs[m], "seq", sibling)
        keep = after(outs[sets + m], pairs[0]) if m else outs[sets]
        pairs.append((keep.astype(F32) + got.astype(F32)).astype(BF))
    def near_side(ids, picked, down_weight):
        send, keep = hidden_grads(True, ids, picked, down_weight)
        return keep, lax.ppermute(send, "seq", sibling)

    def no_near(*_):
        return (jnp.zeros((live_rows, block), BF),) * 2

    keep, got = lax.cond(present, near_side, no_near, after(ids, pairs[-1]), picked, down_weight)
    hidden = keep.astype(F32) + got.astype(F32)
    ds, ds_core, ds_far = [], [], []
    for m in range(sets):
        got = lax.ppermute(pairs[m], "seq", across)
        if m > 0:
            got = after(got, ds[m - 1])
        part = slice(m * set_rows, (m + 1) * set_rows)
        ds.append(jnp.stack(derive(near[0, part], near[1, part], hidden[part] + got.astype(F32))))
        ds_core.append(lax.ppermute(ds[m], "seq", sibling))
        ds_far.append(lax.ppermute(ds[m], "seq", across))
    firsts = near_back(ids, ds, ds_core, gate_weight, up_weight)
    pieces, parts = [], firsts
    for m in range(sets):
        d_both = lax.ppermute(after(ds_far[m], parts[0]), "seq", sibling)
        parts = far_back(ids, place[m].reshape(n * piece, set_rows), ds_far[m], d_both, gate_weight, up_weight, firsts[m])
        total = parts[0].astype(F32)
        for k in (1, 3, 2):
            shift = [(i, (i + k) % n) for i in range(n)]
            total += lax.ppermute(parts[k], "tensor", shift).astype(F32)
        pieces.append(total.astype(BF))
    return jnp.dot(final, jnp.concatenate(pieces), preferred_element_type=F32).astype(BF)


def solution(mesh):
    placed = (
        P(("group", "seq"), "tensor"),
        P(("group", "seq"), "tensor"),
        P(("group", "seq")),
        P("group"),
        P("seq", "tensor"),
        P("seq", "tensor"),
        P("tensor", "seq"),
    )
    if mesh.shape["tensor"] == 4 and mesh.shape["seq"] == 4:
        body = functools.partial(tuned, 4)
    else:
        body = general
    return jax.shard_map(
        body, mesh=mesh, in_specs=placed, out_specs=P(("group", "tensor"), "seq"), check_vma=False
    )
```

```python
import functools
import jax
import jax.numpy as jnp
from jax import lax
from jax.experimental import pallas as pl
from jax.experimental.pallas import tpu as pltpu
from jax.sharding import PartitionSpec as P

BF, F32 = jnp.bfloat16, jnp.float32
ROW_CONTRACT = (((1,), (1,)), ((), ()))
VMEM = 49 * 1024 * 1024
PROJECT_COST, HIDDEN_COST, NEAR_COST, FAR_COST = 20000000, 60000000, 40000000, 40000000


def derive(gate, up, hidden_grad):
    sig = jax.nn.sigmoid(gate)
    d_up = (hidden_grad * gate * sig).astype(BF)
    d_gate = (hidden_grad * up * sig * (1.0 + gate * (1.0 - sig))).astype(BF)
    return (d_gate, d_up)


def general(tokens, grad_out, counts, packing, gate_weight, up_weight, down_weight):
    shard_rows = tokens.shape[0]
    alive_rows = jnp.arange(shard_rows, dtype=jnp.int32) < counts[0]
    masked = jnp.where(alive_rows[:, None], grad_out, jnp.zeros_like(grad_out))
    whole_tokens, whole_cotangent = (
        lax.all_gather(tokens, "tensor", axis=1, tiled=True),
        lax.all_gather(masked, "tensor", axis=1, tiled=True),
    )
    owned_tokens, owned_cotangent = (
        lax.all_to_all(whole_tokens, "seq", split_axis=1, concat_axis=0, tiled=True),
        lax.all_to_all(whole_cotangent, "seq", split_axis=1, concat_axis=0, tiled=True),
    )
    packed_tokens = jnp.take(owned_tokens, packing, axis=0)
    packed_cotangent = jnp.take(owned_cotangent, packing, axis=0)
    gate_part = jnp.dot(packed_tokens, gate_weight, preferred_element_type=F32)
    up_part = jnp.dot(packed_tokens, up_weight, preferred_element_type=F32)
    hidden_part = lax.dot_general(
        packed_cotangent, down_weight, ROW_CONTRACT, preferred_element_type=F32
    )
    gate, up, hidden_grad = (
        lax.psum(gate_part.astype(BF), "seq").astype(F32),
        lax.psum(up_part.astype(BF), "seq").astype(F32),
        lax.psum(hidden_part.astype(BF), "seq").astype(F32),
    )
    d_gate, d_up = derive(gate, up, hidden_grad)
    result = lax.dot_general(d_gate, gate_weight, ROW_CONTRACT, preferred_element_type=F32)
    return lax.psum_scatter(
        (result + lax.dot_general(d_up, up_weight, ROW_CONTRACT, preferred_element_type=F32)).astype(BF),
        "tensor",
        scatter_dimension=0,
        tiled=True,
    )


def region(ref, axis, index, size):
    spot = pl.ds(pl.multiple_of(index * size, size), size)
    return ref.at[spot] if axis == 0 else ref.at[:, spot]


def slot_index(slot, core, x):
    which_core = 1 - core if slot % 2 == 0 else core
    which_x = 1 - x if slot // 2 == 0 else x
    return which_x * 2 + which_core


def start(source, target, sem):
    copy = pltpu.make_async_copy(source, target, sem)
    copy.start()
    return copy


class Stream:
    def __init__(self, copies, ahead):
        self.copies, self.ahead, self.begun = copies, ahead, 0
        self.reach(0)

    def reach(self, index):
        while self.begun < min(index + self.ahead, len(self.copies)):
            for copy in self.copies[self.begun]:
                copy.start()
            self.begun += 1

    def wait(self, index):
        for copy in self.copies[index]:
            copy.wait()
        self.reach(index + 1)


IN_VMEM = pl.BlockSpec(memory_space=pltpu.VMEM)
IN_HBM = pl.BlockSpec(memory_space=pl.ANY)
IN_SMEM = pl.BlockSpec(memory_space=pltpu.SMEM)


def call(kernel, in_specs, out_shape, scratch, cost):
    return pl.pallas_call(
        kernel,
        in_specs=in_specs,
        out_specs=[IN_HBM] * len(out_shape),
        out_shape=[jax.ShapeDtypeStruct(shape, dtype) for shape, dtype in out_shape],
        scratch_shapes=scratch,
        compiler_params=pltpu.CompilerParams(vmem_limit_bytes=VMEM),
        cost_estimate=pl.CostEstimate(flops=0, bytes_accessed=cost, transcendentals=0),
    )


def pick_start(parts, arrived, sems):
    width = parts[0].shape[0]
    return [start(part, arrived.at[pl.ds(k * width, width)], sems.at[k]) for k, part in enumerate(parts)]


def pick_end(moves, select_ref, arrived, rows_v):
    for move in moves:
        move.wait()
    rows_v[...] = jnp.dot(select_ref[...], arrived[...], preferred_element_type=F32).astype(BF)


def project_kernel(near, ids, *refs):
    if near:
        rows_in, gate_w, up_w, send, keep, gate_v, up_v, out_v, rows_v, sems = refs
        moves = [start(rows_in, rows_v, sems.at[0, 0])]
    else:
        select_ref, p0, p1, p2, p3, gate_w, up_w, send, keep, rows_out, gate_v, up_v, out_v, rows_v, arrived, sems = refs
        moves = pick_start((p0, p1, p2, p3), arrived, sems.at[0])
    core, x = ids[0], ids[1]
    block = gate_v.shape[2]
    loads = []
    for i in range(2):
        index = slot_index(2 * near + i, core, x)
        for a, (weight, held) in enumerate(((gate_w, gate_v), (up_w, up_v))):
            loads.append([pltpu.make_async_copy(region(weight, 1, index, block), held.at[i], sems.at[1 + a, i])])
    loads = Stream(loads, 2)
    stores = []
    if near:
        moves[0].wait()
    else:
        pick_end(moves, select_ref, arrived, rows_v)
        stores.append(start(rows_v, rows_out, sems.at[0, 0]))
    for i, out in enumerate((send, keep)):
        for a, held in enumerate((gate_v, up_v)):
            loads.wait(2 * i + a)
            out_v[i, a] = jnp.dot(rows_v[...], held[i], preferred_element_type=F32).astype(BF)
            stores.append(start(out_v.at[i, a], out.at[a], sems.at[3 + a, i]))
    for store in stores:
        store.wait()


def project(near, ids, rows, gate_weight, up_weight):
    depth, block = gate_weight.shape[0], gate_weight.shape[1] // 4
    count = rows.shape[0] if near else rows[0].shape[0]
    args = (rows,) if near else rows
    picked = [] if near else [((count, depth), BF)]
    arrived = [] if near else [pltpu.VMEM((rows[0].shape[1], depth), BF)]
    return call(
        functools.partial(project_kernel, near),
        [IN_SMEM] + [IN_HBM if near else IN_VMEM] + [IN_HBM] * (len(args) + 1),
        [((2, count, block), BF)] * 2 + picked,
        [pltpu.VMEM((2, depth, block), BF)] * 2 + [
            pltpu.VMEM((2, 2, count, block), BF),
            pltpu.VMEM((count, depth), BF),
        ] + arrived + [pltpu.SemaphoreType.DMA((5, 4))],
        PROJECT_COST,
    )(ids, *args, gate_weight, up_weight)


def hidden_kernel(near, ids, *refs):
    if near:
        rows_in, down, send, keep, down_v, out_v, rows_v, sems = refs
        moves = [start(rows_in, rows_v, sems.at[0, 0])]
        outs = ((send,), (keep,))
    else:
        order_ref, *parts, down, o0, o1, o2, o3, rows_out, down_v, out_v, rows_v, sems = refs
        outs = ((o0, o1), (o2, o3))
    core, x = ids[0], ids[1]
    block = down_v.shape[1]
    loads = Stream(
        [[pltpu.make_async_copy(region(down, 0, slot_index(2 * near + i, core, x), block), down_v.at[i], sems.at[1, i])]
         for i in range(2)], 2)
    stores = []
    if near:
        moves[0].wait()
    else:
        total = jnp.dot(order_ref[0], parts[0][...], preferred_element_type=F32)
        for k in range(1, len(parts)):
            total += jnp.dot(order_ref[k], parts[k][...], preferred_element_type=F32)
        rows_v[...] = total.astype(BF)
        stores.append(start(rows_v, rows_out, sems.at[0, 0]))
    for i in range(2):
        loads.wait(i)
        hidden = lax.dot_general(rows_v[...], down_v[i], ROW_CONTRACT, preferred_element_type=F32)
        out_v[i] = hidden.astype(BF)
        for m, out in enumerate(outs[i]):
            rows = out.shape[0]
            stores.append(start(out_v.at[i, pl.ds(m * rows, rows)], out, sems.at[2 + m, i]))
    for store in stores:
        store.wait()


def hidden_grads(near, ids, rows, down_weight):
    depth, block = down_weight.shape[1], down_weight.shape[0] // 4
    count = rows.shape[0] if near else rows[0].shape[1]
    args = (rows,) if near else rows
    outs = [((count, block), BF)] * 2 if near else [((count // 2, block), BF)] * 4 + [((count, depth), BF)]
    return call(
        functools.partial(hidden_kernel, near),
        [IN_SMEM] + [IN_HBM if near else IN_VMEM] * len(args) + [IN_HBM],
        outs,
        [
            pltpu.VMEM((2, block, depth), BF),
            pltpu.VMEM((2, count, block), BF),
            pltpu.VMEM((count, depth), BF),
            pltpu.SemaphoreType.DMA((4, 4)),
        ],
        HIDDEN_COST,
    )(ids, *args, down_weight)


CHUNKS = 4


def back_begin(core, which_x, pairs, gate_w, up_w, grads_v, weight_v, sems, grad_sems):
    rows, block = pairs[0][0].shape[1], pairs[0][0].shape[2]
    height, width = gate_w.shape[0] // CHUNKS, 2 * block
    moves = []
    for m, pair in enumerate(pairs):
        for source, value in enumerate(pair):
            which_core = core if source == 0 else 1 - core
            spot = pl.ds(pl.multiple_of(which_core * block, block), block)
            for a in range(2):
                moves.append(start(value.at[a], grads_v.at[a, pl.ds(m * rows, rows), spot],
                                   grad_sems.at[m, 2 * source + a]))
    side = pl.ds(pl.multiple_of(which_x * width, width), width)
    loads = []
    for chunk in range(CHUNKS):
        high = pl.ds(chunk * height, height)
        loads.append([
            pltpu.make_async_copy(weight.at[high, side], weight_v.at[a, high], sems.at[chunk, a])
            for a, weight in enumerate((gate_w, up_w))
        ])
    return moves, Stream(loads, 2)


def back_chunk(chunk, grads_v, weight_v, loads):
    height = weight_v.shape[1] // CHUNKS
    spot = pl.ds(chunk * height, height)
    loads.wait(chunk)
    total = lax.dot_general(grads_v[0], weight_v[0, spot], ROW_CONTRACT, preferred_element_type=F32)
    return total + lax.dot_general(grads_v[1], weight_v[1, spot], ROW_CONTRACT, preferred_element_type=F32)


def near_kernel(ids, mine_a, other_a, mine_b, other_b, gate_w, up_w, out_a, out_b,
                grads_v, weight_v, out_v, sems, grad_sems, out_sems):
    moves, loads = back_begin(ids[0], ids[1], ((mine_a, other_a), (mine_b, other_b)), gate_w, up_w,
                              grads_v, weight_v, sems, grad_sems)
    height, rows = gate_w.shape[0] // CHUNKS, out_a.shape[0]
    for move in moves:
        move.wait()
    stores = []
    for chunk in range(CHUNKS):
        spot = pl.ds(chunk * height, height)
        out_v[:, spot] = back_chunk(chunk, grads_v, weight_v, loads)
        for m, out in enumerate((out_a, out_b)):
            stores.append(start(out_v.at[pl.ds(m * rows, rows), spot], out.at[:, spot], out_sems.at[chunk, m]))
    for store in stores:
        store.wait()


def far_kernel(ids, place_ref, mine, other, gate_w, up_w, first, o0, o1, o2, o3,
               grads_v, weight_v, first_v, out_v, sems, grad_sems, out_sems, first_sem):
    begun = start(first, first_v, first_sem.at[0])
    moves, loads = back_begin(ids[0], 1 - ids[1], ((mine, other),), gate_w, up_w, grads_v, weight_v, sems, grad_sems)
    height = gate_w.shape[0] // CHUNKS
    piece = o0.shape[0]
    for move in [begun] + moves:
        move.wait()
    stores = []
    for chunk in range(CHUNKS):
        spot = pl.ds(chunk * height, height)
        total = first_v[:, spot] + back_chunk(chunk, grads_v, weight_v, loads)
        out_v[:, spot] = jnp.dot(place_ref[...], total.astype(BF), preferred_element_type=F32).astype(BF)
        for k, out in enumerate((o0, o1, o2, o3)):
            part = out_v.at[pl.ds(k * piece, piece), spot]
            stores.append(start(part, out.at[:, spot], out_sems.at[chunk, k]))
    for store in stores:
        store.wait()


def near_back(ids, mine, other, gate_weight, up_weight):
    sets, rows, block, depth = len(mine), mine[0].shape[1], mine[0].shape[2], gate_weight.shape[0]
    count = sets * rows
    return call(
        near_kernel,
        [IN_SMEM] + [IN_HBM] * 6,
        [((rows, depth), F32)] * 2,
        [
            pltpu.VMEM((2, count, 2 * block), BF),
            pltpu.VMEM((2, depth, 2 * block), BF),
            pltpu.VMEM((count, depth), F32),
            pltpu.SemaphoreType.DMA((CHUNKS, 2)),
            pltpu.SemaphoreType.DMA((sets, 4)),
            pltpu.SemaphoreType.DMA((CHUNKS, sets)),
        ],
        NEAR_COST,
    )(ids, mine[0], other[0], mine[1], other[1], gate_weight, up_weight)


def far_back(ids, place, mine, other, gate_weight, up_weight, first):
    rows, block, depth = mine.shape[1], mine.shape[2], gate_weight.shape[0]
    count = place.shape[0]
    return call(
        far_kernel,
        [IN_SMEM, IN_VMEM] + [IN_HBM] * 5,
        [((count // 4, depth), BF)] * 4,
        [
            pltpu.VMEM((2, rows, 2 * block), BF),
            pltpu.VMEM((2, depth, 2 * block), BF),
            pltpu.VMEM((rows, depth), F32),
            pltpu.VMEM((count, depth), BF),
            pltpu.SemaphoreType.DMA((CHUNKS, 2)),
            pltpu.SemaphoreType.DMA((1, 4)),
            pltpu.SemaphoreType.DMA((CHUNKS, 4)),
            pltpu.SemaphoreType.DMA((1,)),
        ],
        FAR_COST,
    )(ids, place, mine, other, gate_weight, up_weight, first)


def after(value, *others):
    return lax.optimization_barrier((value,) + others)[0]


def tuned(n, tokens, grad_out, counts, packing, gate_weight, up_weight, down_weight):
    shard_rows, depth = tokens.shape
    rows = packing.shape[0]
    live_rows = rows * 3 // 4
    sets, block = 2, gate_weight.shape[1] // 4
    set_rows, piece = live_rows // sets, shard_rows // sets
    t, s = lax.axis_index("tensor"), lax.axis_index("seq")
    core, x = s % 2, s // 2
    ids = jnp.stack([core, x]).astype(jnp.int32)
    sibling = [(i, i ^ 1) for i in range(n)]
    across = [(i, i ^ 2) for i in range(n)]

    def spread(value, k):
        pairs = [(a * n + b, ((b + k) % n) * n + a) for a in range(n) for b in range(n)]
        return lax.ppermute(value, ("tensor", "seq"), pairs)

    token_parts = [spread(tokens, k) for k in range(n)]

    all_counts = lax.all_gather(counts, "seq", tiled=True)
    home, place_in = packing // shard_rows, packing % shard_rows
    bound = jnp.sum(jnp.where(home[:, None] == jnp.arange(n)[None, :], all_counts[None, :], 0), axis=1)
    alive = place_in < bound
    order = jnp.arange(rows, dtype=jnp.int32)
    rank = jnp.sum(jnp.where(order[None, :] < order[:, None], alive[None, :].astype(jnp.int32), 0), axis=1)
    index = jnp.where(alive, (rank % sets) * set_rows + rank // sets, -1)
    slot = jnp.arange(rows, dtype=jnp.int32)
    arriving = ((t - slot // shard_rows) % n) * shard_rows + slot % shard_rows
    to_row = (index[None, :] == jnp.arange(live_rows, dtype=jnp.int32)[:, None]).astype(BF)
    from_slot = (packing[:, None] == arriving[None, :]).astype(BF)
    select = jnp.dot(to_row, from_slot, preferred_element_type=F32).astype(BF)
    before = jnp.sum(
        jnp.where(order[None, :] < (jnp.arange(n) * shard_rows)[:, None], alive[None, :].astype(jnp.int32), 0), axis=1
    )
    begin = jnp.stack([(before + sets - 1 - m) // sets for m in range(sets)])
    target = (t + jnp.arange(n)) % n
    target_begin = jnp.sum(
        jnp.where(target[None, :, None] == jnp.arange(n)[None, None, :], begin[:, None, :], 0), axis=2
    )
    place = (
        target_begin[:, :, None, None] + jnp.arange(piece)[None, None, :, None]
        == jnp.arange(set_rows)[None, None, None, :]
    ).astype(BF)
    own = (order // shard_rows == t)
    mine_rank = jnp.sum(jnp.where((order[None, :] == t * shard_rows + jnp.arange(shard_rows)[:, None]),
                                  jnp.where(alive, rank, -1)[None, :], 0), axis=1)
    spot = jnp.where(mine_rank >= 0, (mine_rank % sets) * piece + mine_rank // sets
                     - jnp.where(mine_rank % sets == 0, target_begin[0, 0], target_begin[1, 0]), -1)
    final = (spot[:, None] == jnp.arange(sets * piece)[None, :]).astype(BF)

    present = all_counts[0] >= 0

    share = live_rows // n
    shards = jnp.stack([s, s ^ 2, s ^ 1, s ^ 3])
    to_share = (index[None, :] == share * s + jnp.arange(share, dtype=jnp.int32)[:, None]).astype(BF)
    local = shards[slot // shard_rows] * shard_rows + slot % shard_rows
    from_local = (packing[:, None] == local[None, :]).astype(BF)
    pick = jnp.dot(to_share, from_local, preferred_element_type=F32).astype(BF)
    came = (t - jnp.arange(n, dtype=jnp.int32)) % n
    order_of = (
        jnp.arange(live_rows, dtype=jnp.int32)[None, :, None]
        == (share * came[:, None] + jnp.arange(share, dtype=jnp.int32)[None, :])[:, None, :]
    ).astype(BF)

    def balance(grad_out, far, pick):
        mine = jnp.concatenate([grad_out, far])
        whole = jnp.concatenate([mine, lax.ppermute(mine, "seq", sibling)])
        return jnp.dot(pick, whole, preferred_element_type=F32).astype(BF)

    def no_balance(*_):
        return jnp.zeros((share, depth), BF)

    held = lax.cond(present, balance, no_balance, grad_out, lax.ppermute(grad_out, "seq", across), pick)
    held = after(held, select, present, order_of, *token_parts)
    grad_parts = [spread(held, k) for k in range(n)]

    def far_side(ids, select, gate_weight, up_weight, *token_parts):
        send, keep, picked = project(False, ids, (select, *token_parts), gate_weight, up_weight)
        got = lax.ppermute(send, "seq", sibling)
        return (keep.astype(F32) + got.astype(F32)).astype(BF), picked

    def absent(*_):
        return jnp.zeros((2, live_rows, block), BF), jnp.zeros((live_rows, depth), BF)

    pair_far, picked = lax.cond(present, far_side, absent, ids, select, gate_weight, up_weight, *token_parts)
    across_near = lax.ppermute(pair_far, "seq", across)

    send, keep = project(True, ids, picked, gate_weight, up_weight)
    *outs, picked = hidden_grads(False, ids, (after(order_of, send), *grad_parts), down_weight)
    near = keep.astype(F32) + lax.ppermute(after(send, outs[0]), "seq", sibling).astype(F32) + across_near.astype(F32)
    pairs = []
    for m in range(sets):
        got = lax.ppermute(outs[m], "seq", sibling)
        keep = after(outs[sets + m], pairs[0]) if m else outs[sets]
        pairs.append((keep.astype(F32) + got.astype(F32)).astype(BF))
    def near_side(ids, picked, down_weight):
        send, keep = hidden_grads(True, ids, picked, down_weight)
        return keep, lax.ppermute(send, "seq", sibling)

    def no_near(*_):
        return (jnp.zeros((live_rows, block), BF),) * 2

    keep, got = lax.cond(present, near_side, no_near, after(ids, pairs[-1]), picked, down_weight)
    hidden = keep.astype(F32) + got.astype(F32)
    ds, ds_core, ds_far = [], [], []
    for m in range(sets):
        got = lax.ppermute(pairs[m], "seq", across)
        if m > 0:
            got = after(got, ds[m - 1])
        part = slice(m * set_rows, (m + 1) * set_rows)
        ds.append(jnp.stack(derive(near[0, part], near[1, part], hidden[part] + got.astype(F32))))
        ds_core.append(lax.ppermute(ds[m], "seq", sibling))
        ds_far.append(lax.ppermute(ds[m], "seq", across))
    ids, final = lax.optimization_barrier((ids, final))
    firsts = near_back(ids, ds, ds_core, gate_weight, up_weight)
    pieces, parts = [], firsts
    for m in range(sets):
        d_both = lax.ppermute(after(ds_far[m], parts[0]), "seq", sibling)
        parts = far_back(ids, place[m].reshape(n * piece, set_rows), ds_far[m], d_both, gate_weight, up_weight, firsts[m])
        total = parts[0].astype(F32)
        for k in (1, 3, 2):
            shift = [(i, (i + k) % n) for i in range(n)]
            total += lax.ppermute(parts[k], "tensor", shift).astype(F32)
        pieces.append(total.astype(BF))
    return jnp.dot(final, jnp.concatenate(pieces), preferred_element_type=F32).astype(BF)


def solution(mesh):
    placed = (
        P(("group", "seq"), "tensor"),
        P(("group", "seq"), "tensor"),
        P(("group", "seq")),
        P("group"),
        P("seq", "tensor"),
        P("seq", "tensor"),
        P("tensor", "seq"),
    )
    if mesh.shape["tensor"] == 4 and mesh.shape["seq"] == 4:
        body = functools.partial(tuned, 4)
    else:
        body = general
    return jax.shard_map(
        body, mesh=mesh, in_specs=placed, out_specs=P(("group", "tensor"), "seq"), check_vma=False
    )
```
